128 devices in a mesh: gx: 32 (over x, y, core), gy: 4 (over z).
Axes of the slice: x: 4, y: 4, z: 4, core: 2. Of those that a mesh axis runs over, the one named last changes fastest.
Arguments:
- conserved: float32 [5, 8, 2048, 2048], P(None, None, 'gx', 'gy'), may hold values from -6 to 6
- solid_cells: int32 [2048, 2048], P('gx', 'gy'), may hold values 0 or 1
- flux_x: float32 [5, 5], replicated, may hold values from -2.5 to 2.5
- flux_y: float32 [5, 5], replicated, may hold values from -2.5 to 2.5
- counts: int32 [128], P(('gx', 'gy')), may hold values from 1 to 576, as said below
- owner_offset: int32 [73728], P(('gx', 'gy')), may hold values from 0 to 8, as said below
- stencil_base: int32 [73728], P(('gx', 'gy')), may hold values from 0 to 31048
- weights: float32 [73728, 16], P(('gx', 'gy')), may hold values from 0 to 0.125
- ghost_cells: int32 [73728], P(('gx', 'gy')), may hold values from 0 to 32767
Outputs:
- advanced: float32 [5, 8, 2048, 2048], P(None, None, 'gx', 'gy')
The draws below stay inside these ranges and needn't reach their ends.
Inputs may be any that keep to these rules, and one draw needn't show every extreme that they name: `owner_offset`: code k names the owner tile at offset (k // 3 - 1, k % 3 - 1) from the sender's tile. Among the 576 rows of one device each code appears exactly 64 times. Live records are the first counts[s] rows of device s. In every draw, some device that is not on the grid's edge has all its eight neighbours and itself at 576.
All inputs are finite; a program needn't handle non-finite values. No bound on the sum of `solid_cells` on one device may be relied on, other than what follows from the above.
Results may differ from the reference program's by a relative error of at most 0.000067.
Values sent between devices are 32-bit elements; how exact they have to be, the bound alone decides.
A program may use at most 128 MiB of HBM per device.

```python
import jax
import jax.numpy as jnp
from jax import lax

CX = 64
CY = 512
NZ = 8
CAP = 64
RP = 576
NX = 2048
NY = 2048
RECORDS = 73728
N_GX = 32
N_GY = 4
DEVICES = 128


def offset_codes(key):
    scores = jax.random.randint(jax.random.fold_in(key, 11), (DEVICES, RP), 0, 1048576)
    order = jnp.argsort(scores, axis=1, stable=True)
    return (order // CAP).astype(jnp.int32).reshape(RECORDS)


def image_layout(key):
    codes = offset_codes(key)
    step_x = codes // 3 - 1
    step_y = codes % 3 - 1
    jitter = jax.random.randint(jax.random.fold_in(key, 12), (4, RECORDS), 0, 3)
    free_x = jax.random.randint(jax.random.fold_in(key, 13), (RECORDS,), 0, CX - 3)
    free_y = jax.random.randint(jax.random.fold_in(key, 14), (RECORDS,), 0, CY - 3)
    base_x = jnp.where(step_x == 1, CX - 4 - jitter[0], jnp.where(step_x == -1, jitter[0], free_x))
    base_y = jnp.where(step_y == 1, CY - 4 - jitter[1], jnp.where(step_y == -1, jitter[1], free_y))
    ghost_x = jnp.where(step_x == 1, jitter[2], jnp.where(step_x == -1, CX - 1 - jitter[2], base_x + jitter[2]))
    ghost_y = jnp.where(step_y == 1, jitter[3], jnp.where(step_y == -1, CY - 1 - jitter[3], base_y + jitter[3]))
    base = (base_x * (CY - 3) + base_y).astype(jnp.int32)
    ghost = (ghost_x * CY + ghost_y).astype(jnp.int32)
    return (base, ghost)


def draw_owner_offset(key, part):
    return offset_codes(key)


def draw_stencil_base(key, part):
    return image_layout(key)[0]


def draw_ghost_cells(key, part):
    return image_layout(key)[1]


def draw_counts(key, part):
    first = jax.random.randint(jax.random.fold_in(key, 21), (DEVICES,), 1, RP + 1)
    second = jax.random.randint(jax.random.fold_in(key, 22), (DEVICES,), 1, RP + 1)
    centre_x = jax.random.randint(jax.random.fold_in(key, 23), (), 1, N_GX - 1)
    centre_y = jax.random.randint(jax.random.fold_in(key, 24), (), 1, N_GY - 1)
    device = jnp.arange(DEVICES, dtype=jnp.int32)
    near = (jnp.abs(device // N_GY - centre_x) <= 1) & (jnp.abs(device % N_GY - centre_y) <= 1)
    return jnp.where(near, RP, jnp.minimum(first, second)).astype(jnp.int32)


def touch_ends(entries, key, least, high):
    longest = entries.shape.index(max(entries.shape))
    spots = []
    for shift in (0, 1):
        where = [jax.random.randint(jax.random.fold_in(key, axis), (), 0, length) for axis, length in enumerate(entries.shape)]
        where[longest] = (where[longest] + shift) % entries.shape[longest]
        spots.append(tuple(where))
    return entries.at[spots[0]].set(least).at[spots[1]].set(high)


def steps_of(own_key, dims, pieces, smallest, largest):
    loudness = 1.0
    for dim, shards_of in pieces:
        heights = jax.random.uniform(jax.random.fold_in(jax.random.fold_in(own_key, 6), dim), (shards_of,), jnp.float32, smallest / len(pieces), largest / len(pieces))
        loudness = loudness * jnp.repeat(jnp.exp(heights), dims[dim] // shards_of).reshape((-1,) + (1,) * (len(dims) - 1 - dim))
    return loudness


def normal_values(own_key, shape, scale, limit, split=(), held_as=jnp.bfloat16):
    entries = jax.random.normal(own_key, shape, jnp.float32) * scale
    if len(split) > 0:
        entries = steps_of(own_key, shape, split, -0.22, 0.18) * entries
    return jnp.clip(entries, min=-limit, max=limit).astype(held_as)


def setup_inputs(seed: int = 0) -> dict:
    splits = jax.random.split(jax.random.key(seed), 10)
    conserved = normal_values(splits[0], (5, NZ, NX, NY), 1.0, 6.0, ((2, 32), (3, 4)), jnp.float32)
    solid_cells = touch_ends((jax.random.randint(splits[1], (NX, NY), 0, 8) < 1).astype(jnp.int32), jax.random.fold_in(splits[1], 1), 0, 1)
    flux_x = normal_values(splits[2], (5, 5), 5 ** -0.5, 2.5, (), jnp.float32)
    flux_y = normal_values(splits[3], (5, 5), 5 ** -0.5, 2.5, (), jnp.float32)
    counts = draw_counts(jax.random.fold_in(splits[9], 71), 0)
    owner_offset = draw_owner_offset(jax.random.fold_in(splits[9], 71), 0)
    stencil_base = draw_stencil_base(jax.random.fold_in(splits[9], 71), 0)
    weights = jnp.clip(0.125 * jax.random.uniform(splits[7], (RECORDS, 16), jnp.float32) ** steps_of(splits[7], (RECORDS, 16), ((0, 128),), -0.2, 0.2), 0.0, 0.125)
    ghost_cells = draw_ghost_cells(jax.random.fold_in(splits[9], 71), 0)
    return dict(conserved=conserved, solid_cells=solid_cells, flux_x=flux_x, flux_y=flux_y, counts=counts, owner_offset=owner_offset, stencil_base=stencil_base, weights=weights, ghost_cells=ghost_cells)


filter_taps = (1.0 / 64, 6.0 / 64, 15.0 / 64, 20.0 / 64, 15.0 / 64, 6.0 / 64, 1.0 / 64)
step_size = 0.25
relax_rate = 0.5
mirror_signs = (1.0, -1.0, -1.0, -1.0, 1.0)


def smooth_along(padded, which_dim, extent):
    running = filter_taps[0] * lax.slice_in_dim(padded, 0, extent, axis=which_dim)
    for offset in range(1, 7):
        running = running + filter_taps[offset] * lax.slice_in_dim(padded, offset, offset + extent, axis=which_dim)
    return running


def smooth(field):
    first = smooth_along(jnp.pad(field, ((0, 0), (0, 0), (3, 3), (0, 0))), 2, field.shape[2])
    return smooth_along(jnp.pad(first, ((0, 0), (0, 0), (0, 0), (3, 3))), 3, field.shape[3])


def reference(conserved, solid_cells, flux_x, flux_y, counts, owner_offset, stencil_base, weights, ghost_cells):
    precise = lax.Precision.HIGHEST
    current = conserved
    for sweep_index in range(3):
        current = current + conserved - smooth(current)
    deconv = current
    widened = jnp.pad(deconv, ((0, 0), (0, 0), (1, 1), (1, 1)))
    slope_x = (widened[:, :, 2:, 1:-1] - widened[:, :, :-2, 1:-1]) * 0.5
    slope_y = (widened[:, :, 1:-1, 2:] - widened[:, :, 1:-1, :-2]) * 0.5
    flux_term = jnp.einsum('fg,gzxy->fzxy', flux_x, slope_x, precision=precise) + jnp.einsum('fg,gzxy->fzxy', flux_y, slope_y, precision=precise)
    sectioned = conserved + step_size * (-flux_term - relax_rate * (deconv - conserved))
    record_index = jnp.arange(owner_offset.shape[0], dtype=jnp.int32)
    source = record_index // RP
    source_x = source // N_GY
    source_y = source % N_GY
    target_x = source_x + owner_offset // 3 - 1
    target_y = source_y + owner_offset % 3 - 1
    inside = (target_x >= 0) & (target_x < N_GX) & (target_y >= 0) & (target_y < N_GY)
    is_used = ((record_index % RP) < counts[source]) & inside
    x_first = source_x * CX + stencil_base // (CY - 3)
    y_first = source_y * CY + stencil_base % (CY - 3)
    tap_offset = jnp.arange(16, dtype=jnp.int32)
    stencil = deconv[:, :, x_first[:, None] + tap_offset // 4, y_first[:, None] + tap_offset % 4]
    used_weights = jnp.where(is_used[:, None], weights, 0.0)
    values = jnp.einsum('fzrt,rt->rfz', stencil, used_weights, precision=precise)
    x_ghost = jnp.clip(target_x, 0, N_GX - 1) * CX + ghost_cells // CY
    y_ghost = jnp.clip(target_y, 0, N_GY - 1) * CY + ghost_cells % CY
    sign_table = jnp.array(mirror_signs, jnp.float32)
    update = sign_table[:, None, None] * jnp.transpose(values, (1, 2, 0))
    contrib = jnp.zeros_like(conserved).at[:, :, x_ghost, y_ghost].add(update)
    return jnp.where(solid_cells[None, None] == 1, 0.0, sectioned) + contrib
```

```python
import functools

import jax
import jax.numpy as jnp
import ml_dtypes
import numpy as np
from jax import lax
from jax.experimental import pallas as pl
from jax.experimental.pallas import tpu as pltpu
from jax.sharding import PartitionSpec as P

F, Z, X, Y = 5, 8, 64, 512
LANES = 128
TILES = Y // LANES
HALO = 10
XE = X + 2 * HALO
ROWS = XE * Z
DROWS = (X + 2) * Z
REC = 576
CAP = 64
SIGNS = (1.0, -1.0, -1.0, -1.0, 1.0)
F32, BF16, I32 = jnp.float32, jnp.bfloat16, jnp.int32
VMEM_BYTES = 60 * 1024 * 1024
OFFSETS = [(k // 3 - 1, k % 3 - 1) for k in range(9)]


def y_matrices(left_edge, right_edge):
    margin = 80
    ys = np.arange(-margin, Y + margin)
    inside = np.ones(ys.shape, bool)
    if left_edge:
        inside &= ys >= 0
    if right_edge:
        inside &= ys < Y
    taps = np.array([1, 6, 15, 20, 15, 6, 1], np.float64) / 64
    single = np.zeros((ys.size, ys.size))
    for offset in range(-3, 4):
        single += np.diag(np.full(ys.size - abs(offset), taps[offset + 3]), offset)
    single = single * inside[:, None] * inside[None, :]
    double = single @ single
    triple = double @ single
    return [-6.0 / 64 * single, 4.0 / 64**2 * double, -1.0 / 64**3 * triple], margin


def block_matrix(powers, margin, y_in, y_out):
    columns = []
    for power in powers:
        full = np.zeros((256, LANES))
        for lane, y in enumerate(y_out):
            if y is not None:
                full[:, lane] = power[y + margin, np.asarray(y_in) + margin]
        columns.append(full)
    return np.concatenate(columns, axis=1)


def filter_constants():
    lane = np.arange(LANES)
    found = []
    for kind in ("mid", "left", "right", "edge_left", "edge_mid", "edge_right"):
        powers, margin = y_matrices(kind.endswith("left"), kind.endswith("right"))
        if kind.startswith("edge"):
            y_in = np.concatenate([np.where(lane < 64, lane, 384 + lane), np.where(lane < 64, Y + lane, lane - 128)])
            y_out = [Y] + [None] * 126 + [-1]
        else:
            c = {"mid": 1, "left": 0, "right": 3}[kind]
            y_in = np.concatenate([128 * c + lane, np.where(lane < 64, 128 * (c + 1) + lane, 128 * (c - 1) + lane)])
            y_out = list(128 * c + lane)
        found.append(block_matrix(powers, margin, np.clip(y_in, -margin, Y + margin - 1), y_out))
    whole = np.stack(found).astype(np.float32)
    high = whole.astype(ml_dtypes.bfloat16)
    low = (whole - high.astype(np.float32)).astype(ml_dtypes.bfloat16)
    first = np.concatenate([high, high], axis=1)[:, :, :128]
    rest = np.concatenate([high, high, low], axis=1)[:, :, 128:]
    return first, rest


def lane_index(rows=8):
    return lax.broadcasted_iota(I32, (rows, LANES), 1)


def prepare_kernel(u_hbm, count_ref, code_ref, base_ref, ghost_ref, weight_ref,
                   low_ref, high_ref, left_ref, right_ref, info_ref, wide_ref, ub, sems):
    copies = [
        pltpu.make_async_copy(u_hbm.at[:, :, pl.ds(c * LANES, LANES)], ub.at[c], sems.at[c]) for c in range(TILES)
    ]
    for copy in copies:
        copy.start()
    code = code_ref[...]
    base = base_ref[...]
    ghost = ghost_ref[...]
    kinds = lax.broadcasted_iota(I32, (16, REC), 0)
    hits = (kinds == code).astype(F32)
    before = (lax.broadcasted_iota(I32, (REC, REC), 0) < lax.broadcasted_iota(I32, (REC, REC), 1)).astype(F32).astype(BF16)
    ahead = jnp.dot(hits.astype(BF16), before, preferred_element_type=F32)
    rank = jnp.sum(ahead * hits, axis=0, keepdims=True).astype(I32)
    slot = code * CAP + rank
    live = lax.broadcasted_iota(I32, (1, REC), 1) < count_ref[0, 0]
    slot = jnp.where(live, slot, REC)
    placing = (lax.broadcasted_iota(I32, (REC, REC), 0) == slot).astype(F32).astype(BF16)
    base_x = ((base.astype(F32) + 0.5) * (1.0 / (Y - 3))).astype(I32)
    base_y = base - base_x * (Y - 3)
    window = jnp.minimum(base_y // 64, 6)
    first_lane = base_y - window * 64
    ghost_y = ghost % Y
    payload_rows = [window, base_x, ghost // Y, ghost_y // LANES, ghost_y % LANES]
    row_id = lax.broadcasted_iota(I32, (8, REC), 0)
    payload = jnp.zeros((8, REC), I32)
    for row, value in enumerate(payload_rows):
        payload = jnp.where(row_id == row, value, payload)
    payload = payload.astype(F32).astype(BF16)
    across = (((1,), (1,)), ((), ()))
    for k in range(9):
        part = lax.dot_general(payload, placing[k * CAP : (k + 1) * CAP], across, preferred_element_type=F32)
        info_ref[k] = jnp.concatenate([part, jnp.zeros((8, LANES - CAP), F32)], axis=1).astype(I32)
    lanes_hit = (lax.broadcasted_iota(I32, (LANES, REC), 0) == first_lane).astype(F32).astype(BF16)
    starts = lax.dot_general(placing, lanes_hit, across, preferred_element_type=F32)
    weight = weight_ref[...]
    weight_a = weight.astype(BF16)
    left_over = weight - weight_a.astype(F32)
    weight_b = left_over.astype(BF16)
    weight_c = (left_over - weight_b.astype(F32)).astype(BF16)
    ordered = (
        jnp.dot(placing, weight_a, preferred_element_type=F32)
        + jnp.dot(placing, weight_b, preferred_element_type=F32)
        + jnp.dot(placing, weight_c, preferred_element_type=F32)
    )
    shifted = [starts] + [pltpu.roll(starts, j, 1) for j in range(1, 4)]
    for i in range(4):
        total = shifted[0] * ordered[:, 4 * i : 4 * i + 1]
        for j in range(1, 4):
            total = total + shifted[j] * ordered[:, 4 * i + j : 4 * i + j + 1]
        wide_ref[i] = total
    for copy in copies:
        copy.wait()
    lane = lane_index()

    def pack(f, carry):
        for c in range(TILES):
            for x in range(HALO):
                low_ref[f, pl.ds(x * 8, 8), pl.ds(c * LANES, LANES)] = ub[c, f, pl.ds(x, 8, stride=X), :]
                high_ref[f, pl.ds(x * 8, 8), pl.ds(c * LANES, LANES)] = ub[c, f, pl.ds(X - HALO + x, 8, stride=X), :]
        for octet in range(8):
            left = jnp.zeros((8, LANES), F32)
            right = jnp.zeros((8, LANES), F32)
            for z in range(Z):
                here = (lane // 16) == z
                row = z * X + octet * 8
                left = jnp.where(here, pltpu.roll(ub[0, f, pl.ds(row, 8), :], 16 * z, 1), left)
                right = jnp.where(
                    here, pltpu.roll(ub[TILES - 1, f, pl.ds(row, 8), :], (16 * z - (LANES - HALO)) % LANES, 1), right
                )
            left_ref[f, pl.ds(octet * 8, 8), :] = left
            right_ref[f, pl.ds(octet * 8, 8), :] = right
        return carry

    lax.fori_loop(0, F, pack, 0)


def neighbour(dx, dy):
    nx, ny = lax.axis_size("gx"), lax.axis_size("gy")
    return (lax.rem(lax.axis_index("gx") + dx + nx, nx), lax.rem(lax.axis_index("gy") + dy + ny, ny))


def greet():
    barrier = pltpu.get_barrier_semaphore()
    for dx, dy in OFFSETS:
        if (dx, dy) != (0, 0):
            pl.semaphore_signal(barrier, inc=1, device_id=neighbour(dx, dy), device_id_type=pl.DeviceIdType.MESH)
    pl.semaphore_wait(barrier, 8)


def exchange_kernel(low_ref, high_ref, left_ref, right_ref, info_ref,
                    xlo, xhi, ylo, yhi, cll, clr, chl, chr_, ghosts, send_sem, recv_sem, own_sem):
    greet()
    plan = [
        (high_ref, xlo, (1, 0)),
        (low_ref, xhi, (-1, 0)),
        (right_ref, ylo, (0, 1)),
        (left_ref, yhi, (0, -1)),
        (right_ref.at[:, pl.ds(X - 16, 16)], cll, (1, 1)),
        (left_ref.at[:, pl.ds(X - 16, 16)], clr, (1, -1)),
        (right_ref.at[:, pl.ds(0, 16)], chl, (-1, 1)),
        (left_ref.at[:, pl.ds(0, 16)], chr_, (-1, -1)),
    ]
    for k, offset in enumerate(OFFSETS):
        if k != 4:
            plan.append((info_ref.at[k], ghosts.at[k], offset))
    copies = []
    for index, (source, target, (dx, dy)) in enumerate(plan):
        copies.append(
            pltpu.make_async_remote_copy(
                src_ref=source, dst_ref=target, send_sem=send_sem.at[index], recv_sem=recv_sem.at[index],
                device_id=neighbour(dx, dy), device_id_type=pl.DeviceIdType.MESH,
            )
        )
    for copy in copies:
        copy.start()
    own = pltpu.make_async_copy(info_ref.at[4], ghosts.at[4], own_sem)
    own.start()
    own.wait()
    for copy in copies:
        copy.wait()


def record_kernel(values_ref, arrived, send_sem, recv_sem, own_sem):
    greet()
    copies = []
    for k, (dx, dy) in enumerate(OFFSETS):
        if k != 4:
            copies.append(
                pltpu.make_async_remote_copy(
                    src_ref=values_ref.at[k], dst_ref=arrived.at[k], send_sem=send_sem.at[k], recv_sem=recv_sem.at[k],
                    device_id=neighbour(dx, dy), device_id_type=pl.DeviceIdType.MESH,
                )
            )
    for copy in copies:
        copy.start()
    own = pltpu.make_async_copy(values_ref.at[4], arrived.at[4], own_sem)
    own.start()
    own.wait()
    for copy in copies:
        copy.wait()


class Binomial:
    def __init__(self):
        self.held = [None] * 6

    def push(self, value):
        for i in range(6):
            before, self.held[i] = self.held[i], value
            if before is None:
                return None
            value = before + value
        return value


def main_kernel(flags, flux_x, flux_y, info, u_hbm, solid_ref, xlo, xhi, ylo, yhi, cll, clr, chl, chr_,
                first_hbm, rest_hbm, wide_ref, section_ref, values_ref,
                ub, firsts, rests, ut, hs, hi_main, lo_main, hi_side, lo_side, vs, dg, de, sems):
    gx, gy = lax.axis_index("gx"), lax.axis_index("gy")
    last_x, last_y = lax.axis_size("gx") - 1, lax.axis_size("gy") - 1
    flag_lo, flag_hi, flag_left, flag_right = flags[0], flags[1], flags[2], flags[3]
    kinds = [
        jnp.where(gy == 0, 1, 0),
        0,
        jnp.where(gy == last_y, 2, 0),
        jnp.where(gy == 0, 3, jnp.where(gy == last_y, 5, 4)),
    ]
    copies = [
        pltpu.make_async_copy(u_hbm.at[:, :, pl.ds(c * LANES, LANES)], ub.at[c], sems.at[c]) for c in range(TILES)
    ]
    for i, kind in enumerate(kinds):
        copies.append(pltpu.make_async_copy(first_hbm.at[kind], firsts.at[i], sems.at[4 + i]))
        copies.append(pltpu.make_async_copy(rest_hbm.at[kind], rests.at[i], sems.at[8 + i]))
    for copy in copies:
        copy.start()
    for copy in copies:
        copy.wait()
    lane = lane_index()
    low_half = lane < 64

    def per_field(f, carry):
        for c in range(TILES):
            ut[c, pl.ds(0, 80), :] = xlo[f, :, pl.ds(c * LANES, LANES)] * flag_lo
            ut[c, pl.ds(ROWS - 80, 80), :] = xhi[f, :, pl.ds(c * LANES, LANES)] * flag_hi
            for x in range(X):
                ut[c, pl.ds((HALO + x) * 8, 8), :] = ub[c, f, pl.ds(x, 8, stride=X), :]
        for octet in range(-2, 10):
            if octet < 0:
                left, right = [r[f, pl.ds((octet + 2) * 8, 8), :] * flag_lo for r in (cll, clr)]
            elif octet >= 8:
                left, right = [r[f, pl.ds((octet - 8) * 8, 8), :] * flag_hi for r in (chl, chr_)]
            else:
                left, right = [r[f, pl.ds(octet * 8, 8), :] for r in (ylo, yhi)]
            left, right = left * flag_left, right * flag_right
            for z in range(Z):
                from_right = pltpu.roll(right, (-16 * z) % LANES, 1)
                from_left = pltpu.roll(left, (LANES - HALO - 16 * z) % LANES, 1)
                hs[pl.ds((octet + 2) * 64 + z, 8, stride=8), :] = jnp.where(low_half, from_right, from_left)

        keep_low = (lane_index(16) < 64).astype(F32).astype(BF16)
        keep_high = (lane_index(16) >= 64).astype(F32).astype(BF16)
        for block in range(ROWS // 16):
            rows = pl.ds(block * 16, 16)
            highs, lows = [], []
            for c in range(TILES + 1):
                value = ut[c, rows, :] if c < TILES else hs[pl.ds(block * 16 + 48, 16), :]
                high = value.astype(BF16)
                low = (value - high.astype(F32)).astype(BF16)
                highs.append(high)
                lows.append(low)
            for parts, main, side in ((highs, hi_main, hi_side), (lows, lo_main, lo_side)):
                lo_parts = [p * keep_low for p in parts]
                hi_parts = [p * keep_high for p in parts]
                for c in range(TILES):
                    main[c, rows, :] = parts[c]
                    after = lo_parts[c + 1] if c < TILES - 1 else lo_parts[TILES]
                    ahead = hi_parts[c - 1] if c > 0 else hi_parts[TILES]
                    side[c, rows, :] = after + ahead
                main[TILES, rows, :] = lo_parts[0] + hi_parts[TILES - 1]
                side[TILES, rows, :] = parts[TILES]

        for c in range(TILES + 1):
            which = (0, 1, 1, 2, 3)[c]
            high = jnp.concatenate([hi_main[c], hi_side[c]], axis=1)
            low = jnp.concatenate([lo_main[c], lo_side[c]], axis=1)
            vs[c % 2, :, pl.ds(0, 128)] = jnp.dot(
                jnp.concatenate([high, low], axis=1), firsts[which], preferred_element_type=F32
            )
            vs[c % 2, :, pl.ds(128, 256)] = jnp.dot(
                jnp.concatenate([high, low, high], axis=1), rests[which], preferred_element_type=F32
            )
            stages = [Binomial(), Binomial(), Binomial()]

            def mask(value, e):
                return value * flag_lo if e < HALO else value * flag_hi if e >= HALO + X else value

            for e in range(XE):
                value = stages[2].push(vs[c % 2, pl.ds(e * 8, 8), pl.ds(256, 128)])
                if value is None:
                    continue
                value = mask(value, e - 3) + vs[c % 2, pl.ds((e - 3) * 8, 8), pl.ds(128, 128)]
                value = stages[1].push(value)
                if value is None:
                    continue
                value = mask(value, e - 6) + vs[c % 2, pl.ds((e - 6) * 8, 8), pl.ds(0, 128)]
                value = stages[0].push(value)
                if value is None:
                    continue
                at = e - 9
                start = ut[c, pl.ds(at * 8, 8), :] if c < TILES else hs[pl.ds(at * 8 + 48, 8), :]
                value = mask(value, at) + 4.0 * start
                drows = pl.ds((at - 9) * 8, 8)
                if c == TILES:
                    de[f, drows, :] = value
                else:
                    dg[2 * c, f, drows, :] = value
        for x in range(1, X + 1):
            drows = pl.ds(x * 8, 8)
            turned = [pltpu.roll(dg[2 * c, f, drows, :], 64, 1) for c in range(TILES)]
            for c in range(TILES - 1):
                dg[2 * c + 1, f, drows, :] = jnp.where(low_half, turned[c], turned[c + 1])
        return carry

    lax.fori_loop(0, F, per_field, 0)

    def per_code(k, carry):
        def per_group(group, held):
            held = list(held)
            weights = [wide_ref[i, pl.ds(pl.multiple_of(k * CAP + group * 8, 8), 8), :] for i in range(4)]
            for j in range(8):
                slot = group * 8 + j
                window = info[k, 0, slot]
                start = pl.multiple_of((info[k, 1, slot] + 1) * 8, 8)
                rows = [jnp.broadcast_to(weights[i][j : j + 1, :], (8, LANES)) for i in range(4)]
                for f in range(F):
                    cells = dg[window, f, pl.ds(start, 32), :]
                    total = cells[0:8] * rows[0]
                    for i in range(1, 4):
                        total = total + cells[8 * i : 8 * i + 8] * rows[i]
                    value = jnp.sum(total, axis=1, keepdims=True) * SIGNS[f]
                    held[f] = jnp.where(lane == slot, value, held[f])
            return tuple(held)

        held = lax.fori_loop(0, CAP // 8, per_group, tuple(jnp.zeros((8, LANES), F32) for _ in range(F)))
        for f in range(F):
            values_ref[k, pl.ds(f * 8, 8), :] = held[f]
        return carry

    lax.fori_loop(0, 9, per_code, 0)

    def per_octet(octet, carry):
        for c in range(TILES):
            solid = solid_ref[pl.ds(pl.multiple_of(octet * 8, 8), 8), pl.ds(c * LANES, LANES)]
            for half in range(4):
                first = pl.multiple_of((octet * 8 + half * 2) * 8, 8)
                here = pl.ds(first + 8, 16)
                slopes_x, slopes_y, mids = [], [], []
                wide_lane = lane_index(16)
                for g in range(F):
                    mid = dg[2 * c, g, here, :]
                    before = dg[2 * c, g, pl.ds(first, 16), :]
                    after = dg[2 * c, g, pl.ds(first + 16, 16), :]
                    left = dg[2 * (c - 1), g, here, :] if c > 0 else de[g, here, :]
                    right = dg[2 * (c + 1), g, here, :] if c < TILES - 1 else de[g, here, :]
                    up = jnp.where(wide_lane == LANES - 1, pltpu.roll(right, LANES - 1, 1), pltpu.roll(mid, LANES - 1, 1))
                    down = jnp.where(wide_lane == 0, pltpu.roll(left, 1, 1), pltpu.roll(mid, 1, 1))
                    mids.append(mid)
                    slopes_x.append(after - before)
                    slopes_y.append(up - down)
                for f in range(F):
                    total = -0.125 * mids[f]
                    for g in range(F):
                        total = total + flux_x[f, g] * slopes_x[g] + flux_y[f, g] * slopes_y[g]
                    for i in range(2):
                        x = octet * 8 + half * 2 + i
                        cells = total[8 * i : 8 * i + 8] + 1.125 * ub[c, f, pl.ds(x, 8, stride=X), :]
                        row = half * 2 + i
                        blocked = jnp.broadcast_to(solid[row : row + 1, :], (8, LANES)) == 1
                        section_ref[c, f, pl.ds(first + 8 * i, 8), :] = jnp.where(blocked, 0.0, cells)
        return carry

    lax.fori_loop(0, X // 8, per_octet, 0)


def scatter_kernel(valid, info, section_ref, arrived, out_hbm, work, natural, sems):
    lane = lane_index()
    for c in range(TILES):
        for f in range(F):
            work[c, f] = section_ref[c, f]

    def per_code(k, carry):
        weight = valid[k]
        blocks = [arrived[k, pl.ds(f * 8, 8), :] * weight for f in range(F)]
        for j in range(CAP):
            start = pl.multiple_of(info[k, 2, j] * 8, 8)
            tile = info[k, 3, j]
            hit = lane == info[k, 4, j]
            for f in range(F):
                value = jnp.broadcast_to(blocks[f][:, j : j + 1], (8, LANES))
                rows = pl.ds(start, 8)
                work[tile, f, rows, :] = work[tile, f, rows, :] + jnp.where(hit, value, 0.0)
        return carry

    lax.fori_loop(0, 9, per_code, 0)
    copies = []
    for c in range(TILES):

        def per_field(f, carry):
            for x in range(X):
                natural[c, f, pl.ds(x, 8, stride=X), :] = work[c, f, pl.ds(x * 8, 8), :]
            return carry

        lax.fori_loop(0, F, per_field, 0)
        copy = pltpu.make_async_copy(natural.at[c], out_hbm.at[:, :, pl.ds(c * LANES, LANES)], sems.at[c])
        copy.start()
        copies.append(copy)
    for copy in copies:
        copy.wait()


def space(kind, count):
    return [pl.BlockSpec(memory_space=kind)] * count


def shards(conserved, solid_cells, flux_x, flux_y, counts, owner_offset, stencil_base, weights, ghost_cells,
           first_matrix, rest_matrix):
    shape = jax.ShapeDtypeStruct
    gx, gy = lax.axis_index("gx"), lax.axis_index("gy")
    nx, ny = lax.axis_size("gx"), lax.axis_size("gy")
    u = conserved.reshape(F, Z * X, Y)
    vmem, smem, anywhere = pltpu.VMEM, pltpu.SMEM, pl.ANY
    low, high, left, right, info, wide = pl.pallas_call(
        prepare_kernel,
        out_shape=[
            shape((F, HALO * 8, Y), F32), shape((F, HALO * 8, Y), F32),
            shape((F, X, LANES), F32), shape((F, X, LANES), F32),
            shape((9, 8, LANES), I32), shape((4, REC, LANES), F32),
        ],
        in_specs=space(anywhere, 1) + space(smem, 1) + space(vmem, 4),
        out_specs=space(vmem, 6),
        scratch_shapes=[pltpu.VMEM((TILES, F, Z * X, LANES), F32), pltpu.SemaphoreType.DMA((TILES,))],
        compiler_params=pltpu.CompilerParams(vmem_limit_bytes=VMEM_BYTES),
        name="prepare",
    )(u, counts.reshape(1, 1), owner_offset.reshape(1, REC), stencil_base.reshape(1, REC), ghost_cells.reshape(1, REC), weights)
    halos = pl.pallas_call(
        exchange_kernel,
        out_shape=[shape((F, HALO * 8, Y), F32)] * 2 + [shape((F, X, LANES), F32)] * 2
        + [shape((F, 16, LANES), F32)] * 4 + [shape((9, 8, LANES), I32)],
        in_specs=space(vmem, 5),
        out_specs=space(vmem, 9),
        scratch_shapes=[pltpu.SemaphoreType.DMA((16,)), pltpu.SemaphoreType.DMA((16,)), pltpu.SemaphoreType.DMA],
        compiler_params=pltpu.CompilerParams(collective_id=0, has_side_effects=True, vmem_limit_bytes=VMEM_BYTES),
        name="halo",
    )(low, high, left, right, info)
    ghosts = halos[8]
    flags = jnp.stack([gx > 0, gx < nx - 1, gy > 0, gy < ny - 1]).astype(F32)
    section, values = pl.pallas_call(
        main_kernel,
        out_shape=[shape((TILES, F, X * Z, LANES), F32), shape((9, F * Z, LANES), F32)],
        in_specs=space(smem, 4) + space(anywhere, 1) + space(vmem, 9) + space(anywhere, 2) + space(vmem, 1),
        out_specs=space(vmem, 2),
        scratch_shapes=[
            pltpu.VMEM((TILES, F, Z * X, LANES), F32),
            pltpu.VMEM((4, 512, 128), BF16), pltpu.VMEM((4, 768, 256), BF16),
            pltpu.VMEM((TILES, ROWS, LANES), F32), pltpu.VMEM((768, LANES), F32),
        ] + [pltpu.VMEM((TILES + 1, ROWS, LANES), BF16)] * 4 + [
            pltpu.VMEM((2, ROWS, 384), F32),
            pltpu.VMEM((7, F, DROWS, LANES), F32), pltpu.VMEM((F, DROWS, LANES), F32),
            pltpu.SemaphoreType.DMA((12,)),
        ],
        compiler_params=pltpu.CompilerParams(vmem_limit_bytes=VMEM_BYTES),
        name="section",
    )(flags, flux_x * -0.125, flux_y * -0.125, info, u, solid_cells, *halos[:8], first_matrix, rest_matrix, wide)
    arrived = pl.pallas_call(
        record_kernel,
        out_shape=shape((9, F * Z, LANES), F32),
        in_specs=space(vmem, 1),
        out_specs=pl.BlockSpec(memory_space=vmem),
        scratch_shapes=[pltpu.SemaphoreType.DMA((9,)), pltpu.SemaphoreType.DMA((9,)), pltpu.SemaphoreType.DMA],
        compiler_params=pltpu.CompilerParams(collective_id=1, has_side_effects=True, vmem_limit_bytes=VMEM_BYTES),
        name="records",
    )(values)
    sources = [(gx - dx, gy - dy) for dx, dy in OFFSETS]
    valid = jnp.stack([(sx >= 0) & (sx < nx) & (sy >= 0) & (sy < ny) for sx, sy in sources]).astype(F32)
    out = pl.pallas_call(
        scatter_kernel,
        out_shape=shape((F, Z * X, Y), F32),
        in_specs=space(smem, 2) + space(vmem, 2),
        out_specs=pl.BlockSpec(memory_space=anywhere),
        scratch_shapes=[
            pltpu.VMEM((TILES, F, X * Z, LANES), F32), pltpu.VMEM((TILES, F, Z * X, LANES), F32),
            pltpu.SemaphoreType.DMA((TILES,)),
        ],
        compiler_params=pltpu.CompilerParams(vmem_limit_bytes=VMEM_BYTES),
        name="scatter",
    )(valid, ghosts, section, arrived)
    return out.reshape(F, Z, X, Y)


def solution(mesh):
    first, rest = filter_constants()

    def advance(*arguments):
        run = jax.shard_map(
            shards,
            mesh=mesh,
            in_specs=(
                P(None, None, "gx", "gy"), P("gx", "gy"), P(), P(), P(("gx", "gy")), P(("gx", "gy")),
                P(("gx", "gy")), P(("gx", "gy"), None), P(("gx", "gy")), P(), P(),
            ),
            out_specs=P(None, None, "gx", "gy"),
            check_vma=False,
        )
        return run(*arguments, jnp.asarray(first), jnp.asarray(rest))

    return advance
```

```python
import functools

import jax
import jax.numpy as jnp
import ml_dtypes
import numpy as np
from jax import lax
from jax.experimental import pallas as pl
from jax.experimental.pallas import tpu as pltpu
from jax.sharding import PartitionSpec as P

F, Z, X, Y = 5, 8, 64, 512
LANES = 128
TILES = Y // LANES
HALO = 10
XE = X + 2 * HALO
ROWS = XE * Z
REC = 576
CAP = 64
SIGNS = (1.0, -1.0, -1.0, -1.0, 1.0)
F32, BF16, I32 = jnp.float32, jnp.bfloat16, jnp.int32
VMEM_BYTES = 60 * 1024 * 1024
OFFSETS = [(k // 3 - 1, k % 3 - 1) for k in range(9)]


def y_matrices(left_edge, right_edge):
    margin = 80
    ys = np.arange(-margin, Y + margin)
    inside = np.ones(ys.shape, bool)
    if left_edge:
        inside &= ys >= 0
    if right_edge:
        inside &= ys < Y
    taps = np.array([1, 6, 15, 20, 15, 6, 1], np.float64) / 64
    single = np.zeros((ys.size, ys.size))
    for offset in range(-3, 4):
        single += np.diag(np.full(ys.size - abs(offset), taps[offset + 3]), offset)
    single = single * inside[:, None] * inside[None, :]
    double = single @ single
    triple = double @ single
    return [-6.0 / 64 * single, 4.0 / 64**2 * double, -1.0 / 64**3 * triple], margin


def block_matrix(powers, margin, y_in, y_out):
    columns = []
    for power in powers:
        full = np.zeros((256, LANES))
        for lane, y in enumerate(y_out):
            if y is not None:
                full[:, lane] = power[y + margin, np.asarray(y_in) + margin]
        columns.append(full)
    return np.concatenate(columns, axis=1)


def filter_constants():
    lane = np.arange(LANES)
    found = []
    for kind in ("mid", "left", "right", "edge_left", "edge_mid", "edge_right"):
        powers, margin = y_matrices(kind.endswith("left"), kind.endswith("right"))
        if kind.startswith("edge"):
            y_in = np.concatenate([np.where(lane < 64, lane, 384 + lane), np.where(lane < 64, Y + lane, lane - 128)])
            y_out = [Y] + [None] * 126 + [-1]
        else:
            c = {"mid": 1, "left": 0, "right": 3}[kind]
            y_in = np.concatenate([128 * c + lane, np.where(lane < 64, 128 * (c + 1) + lane, 128 * (c - 1) + lane)])
            y_out = list(128 * c + lane)
        found.append(block_matrix(powers, margin, np.clip(y_in, -margin, Y + margin - 1), y_out))
    whole = np.stack(found).astype(np.float32)
    high = whole.astype(ml_dtypes.bfloat16)
    low = (whole - high.astype(np.float32)).astype(ml_dtypes.bfloat16)
    first = np.concatenate([high, high], axis=1)[:, :, :128]
    rest = np.concatenate([high, high, low], axis=1)[:, :, 128:]
    return first, rest


def lane_index(rows=8):
    return lax.broadcasted_iota(I32, (rows, LANES), 1)


def prepare_kernel(count_ref, code_ref, base_ref, ghost_ref, weight_ref, info_ref, wide_ref):
    code = code_ref[...].reshape(1, REC)
    base = base_ref[...].reshape(1, REC)
    ghost = ghost_ref[...].reshape(1, REC)
    kinds = lax.broadcasted_iota(I32, (16, REC), 0)
    hits = (kinds == code).astype(F32)
    before = (lax.broadcasted_iota(I32, (REC, REC), 0) < lax.broadcasted_iota(I32, (REC, REC), 1)).astype(F32).astype(BF16)
    ahead = jnp.dot(hits.astype(BF16), before, preferred_element_type=F32)
    rank = jnp.sum(ahead * hits, axis=0, keepdims=True).astype(I32)
    slot = code * CAP + rank
    live = lax.broadcasted_iota(I32, (1, REC), 1) < count_ref[0]
    slot = jnp.where(live, slot, REC)
    placing = (lax.broadcasted_iota(I32, (REC, REC), 0) == slot).astype(F32).astype(BF16)
    base_x = ((base.astype(F32) + 0.5) * (1.0 / (Y - 3))).astype(I32)
    base_y = base - base_x * (Y - 3)
    window = jnp.minimum(base_y // 64, 6)
    first_lane = base_y - window * 64
    ghost_y = ghost % Y
    payload_rows = [window, base_x, ghost // Y, ghost_y // LANES, ghost_y % LANES]
    row_id = lax.broadcasted_iota(I32, (8, REC), 0)
    payload = jnp.zeros((8, REC), I32)
    for row, value in enumerate(payload_rows):
        payload = jnp.where(row_id == row, value, payload)
    payload = payload.astype(F32).astype(BF16)
    across = (((1,), (1,)), ((), ()))
    for k in range(9):
        part = lax.dot_general(payload, placing[k * CAP : (k + 1) * CAP], across, preferred_element_type=F32)
        info_ref[k] = jnp.concatenate([part, jnp.zeros((8, LANES - CAP), F32)], axis=1).astype(I32)
    lanes_hit = (lax.broadcasted_iota(I32, (LANES, REC), 0) == first_lane).astype(F32).astype(BF16)
    starts = lax.dot_general(placing, lanes_hit, across, preferred_element_type=F32)
    weight = weight_ref[...]
    weight_a = weight.astype(BF16)
    left_over = weight - weight_a.astype(F32)
    weight_b = left_over.astype(BF16)
    weight_c = (left_over - weight_b.astype(F32)).astype(BF16)
    ordered = sum(
        lax.dot_general(placing, part, across, preferred_element_type=F32) for part in (weight_a, weight_b, weight_c)
    )
    shifted = [starts] + [pltpu.roll(starts, j, 1) for j in range(1, 4)]
    for i in range(4):
        total = shifted[0] * ordered[:, 4 * i : 4 * i + 1]
        for j in range(1, 4):
            total = total + shifted[j] * ordered[:, 4 * i + j : 4 * i + j + 1]
        wide_ref[i] = total


def neighbour(dx, dy):
    nx, ny = lax.axis_size("gx"), lax.axis_size("gy")
    return (lax.rem(lax.axis_index("gx") + dx + nx, nx), lax.rem(lax.axis_index("gy") + dy + ny, ny))


def signal_neighbours():
    barrier = pltpu.get_barrier_semaphore()
    for dx, dy in OFFSETS:
        if (dx, dy) != (0, 0):
            pl.semaphore_signal(barrier, inc=1, device_id=neighbour(dx, dy), device_id_type=pl.DeviceIdType.MESH)


def wait_neighbours():
    pl.semaphore_wait(pltpu.get_barrier_semaphore(), 8)


class Binomial:
    def __init__(self):
        self.held = [None] * 6

    def push(self, value):
        for i in range(6):
            before, self.held[i] = self.held[i], value
            if before is None:
                return None
            value = before + value
        return value


def remote(source, target, send_sem, recv_sem, offset):
    return pltpu.make_async_remote_copy(
        src_ref=source, dst_ref=target, send_sem=send_sem, recv_sem=recv_sem,
        device_id=neighbour(*offset), device_id_type=pl.DeviceIdType.MESH,
    )


def main_kernel(flux_x, flux_y, info, u_hbm, info_hbm, solid_ref, first_hbm, rest_hbm, wide_ref,
                section_hbm, arrived, ghosts,
                ub, firsts, rests, ut, hs, hi_main, lo_main, hi_side, lo_side, vs, dg, de, section_ref, values_ref,
                low_ref, high_ref, left_ref, right_ref, xlo, xhi, ylo, yhi, cll, clr, chl, chr_,
                sems, row_send, row_recv, side_send, side_recv, record_send, record_recv, out_sems):
    signal_neighbours()
    gx, gy = lax.axis_index("gx"), lax.axis_index("gy")
    last_x, last_y = lax.axis_size("gx") - 1, lax.axis_size("gy") - 1
    flag_lo = jnp.where(gx > 0, 1.0, 0.0).astype(F32)
    flag_hi = jnp.where(gx < last_x, 1.0, 0.0).astype(F32)
    flag_left = jnp.where(gy > 0, 1.0, 0.0).astype(F32)
    flag_right = jnp.where(gy < last_y, 1.0, 0.0).astype(F32)
    kinds = [
        jnp.where(gy == 0, 1, 0),
        0,
        jnp.where(gy == last_y, 2, 0),
        jnp.where(gy == 0, 3, jnp.where(gy == last_y, 5, 4)),
    ]
    copies = [
        pltpu.make_async_copy(u_hbm.at[:, :, pl.ds(c * LANES, LANES)], ub.at[c], sems.at[c]) for c in range(TILES)
    ]
    constant_copies = []
    for i, kind in enumerate(kinds):
        constant_copies.append(pltpu.make_async_copy(first_hbm.at[kind], firsts.at[i], sems.at[4 + i]))
        constant_copies.append(pltpu.make_async_copy(rest_hbm.at[kind], rests.at[i], sems.at[8 + i]))
    for copy in copies + constant_copies:
        copy.start()
    for copy in copies:
        copy.wait()
    lane = lane_index()
    low_half = lane < 64

    def pack_rows(f, carry):
        for c in range(TILES):
            for x in range(HALO):
                low_ref[f, pl.ds(x * 8, 8), pl.ds(c * LANES, LANES)] = ub[c, f, pl.ds(x, 8, stride=X), :]
                high_ref[f, pl.ds(x * 8, 8), pl.ds(c * LANES, LANES)] = ub[c, f, pl.ds(X - HALO + x, 8, stride=X), :]
        return carry

    lax.fori_loop(0, F, pack_rows, 0)
    wait_neighbours()

    def row_copies(f):
        return (
            remote(high_ref.at[f], xlo.at[f], row_send.at[0, f], row_recv.at[0, f], (1, 0)),
            remote(low_ref.at[f], xhi.at[f], row_send.at[1, f], row_recv.at[1, f], (-1, 0)),
        )

    for f in range(F):
        for copy in row_copies(f):
            copy.start()

    def pack_sides(f, carry):
        for octet in range(8):
            left = jnp.zeros((8, LANES), F32)
            right = jnp.zeros((8, LANES), F32)
            for z in range(Z):
                here = (lane // 16) == z
                row = z * X + octet * 8
                left = jnp.where(here, pltpu.roll(ub[0, f, pl.ds(row, 8), :], 16 * z, 1), left)
                right = jnp.where(
                    here, pltpu.roll(ub[TILES - 1, f, pl.ds(row, 8), :], (16 * z - (LANES - HALO)) % LANES, 1), right
                )
            left_ref[f, pl.ds(octet * 8, 8), :] = left
            right_ref[f, pl.ds(octet * 8, 8), :] = right
        return carry

    lax.fori_loop(0, F, pack_sides, 0)
    plan = [
        (right_ref, ylo, (0, 1)),
        (left_ref, yhi, (0, -1)),
        (right_ref.at[:, pl.ds(X - 16, 16)], cll, (1, 1)),
        (left_ref.at[:, pl.ds(X - 16, 16)], clr, (1, -1)),
        (right_ref.at[:, pl.ds(0, 16)], chl, (-1, 1)),
        (left_ref.at[:, pl.ds(0, 16)], chr_, (-1, -1)),
    ]
    for k, offset in enumerate(OFFSETS):
        if k != 4:
            plan.append((info_hbm.at[k], ghosts.at[k], offset))
    side_copies = [
        remote(source, target, side_send.at[index], side_recv.at[index], offset)
        for index, (source, target, offset) in enumerate(plan)
    ]
    for copy in side_copies:
        copy.start()
    own_ghosts = pltpu.make_async_copy(info_hbm.at[4], ghosts.at[4], out_sems.at[0])
    own_ghosts.start()

    def turn(f, carry):
        for c in range(TILES):
            for x in range(X):
                ut[f, c, pl.ds((HALO + x) * 8, 8), :] = ub[c, f, pl.ds(x, 8, stride=X), :]
        return carry

    lax.fori_loop(0, F, turn, 0)
    for copy in constant_copies:
        copy.wait()
    for copy in side_copies:
        copy.wait_recv()

    def per_field(f, carry):
        for copy in row_copies(f):
            copy.wait_recv()
        for c in range(TILES):
            ut[f, c, pl.ds(0, 80), :] = xlo[f, :, pl.ds(c * LANES, LANES)] * flag_lo
            ut[f, c, pl.ds(ROWS - 80, 80), :] = xhi[f, :, pl.ds(c * LANES, LANES)] * flag_hi
        for octet in range(-2, 10):
            if octet < 0:
                left, right = [r[f, pl.ds((octet + 2) * 8, 8), :] * flag_lo for r in (cll, clr)]
            elif octet >= 8:
                left, right = [r[f, pl.ds((octet - 8) * 8, 8), :] * flag_hi for r in (chl, chr_)]
            else:
                left, right = [r[f, pl.ds(octet * 8, 8), :] for r in (ylo, yhi)]
            left, right = left * flag_left, right * flag_right
            for z in range(Z):
                from_right = pltpu.roll(right, (-16 * z) % LANES, 1)
                from_left = pltpu.roll(left, (LANES - HALO - 16 * z) % LANES, 1)
                hs[pl.ds((octet + 2) * 64 + z, 8, stride=8), :] = jnp.where(low_half, from_right, from_left)

        keep_low = (lane_index(16) < 64).astype(F32).astype(BF16)
        keep_high = (lane_index(16) >= 64).astype(F32).astype(BF16)
        for block in range(ROWS // 16):
            rows = pl.ds(block * 16, 16)
            highs, lows = [], []
            for c in range(TILES + 1):
                value = ut[f, c, rows, :] if c < TILES else hs[pl.ds(block * 16 + 48, 16), :]
                high = value.astype(BF16)
                low = (value - high.astype(F32)).astype(BF16)
                highs.append(high)
                lows.append(low)
            for parts, main, side in ((highs, hi_main, hi_side), (lows, lo_main, lo_side)):
                lo_parts = [p * keep_low for p in parts]
                hi_parts = [p * keep_high for p in parts]
                for c in range(TILES):
                    main[c, rows, :] = parts[c]
                    after = lo_parts[c + 1] if c < TILES - 1 else lo_parts[TILES]
                    ahead = hi_parts[c - 1] if c > 0 else hi_parts[TILES]
                    side[c, rows, :] = after + ahead
                main[TILES, rows, :] = lo_parts[0] + hi_parts[TILES - 1]
                side[TILES, rows, :] = parts[TILES]

        for c in range(TILES + 1):
            which = (0, 1, 1, 2, 3)[c]
            high = jnp.concatenate([hi_main[c], hi_side[c]], axis=1)
            low = jnp.concatenate([lo_main[c], lo_side[c]], axis=1)
            vs[c % 2, :, pl.ds(0, 128)] = jnp.dot(
                jnp.concatenate([high, low], axis=1), firsts[which], preferred_element_type=F32
            )
            vs[c % 2, :, pl.ds(128, 256)] = jnp.dot(
                jnp.concatenate([high, low, high], axis=1), rests[which], preferred_element_type=F32
            )
            stages = [Binomial(), Binomial(), Binomial()]

            def mask(value, e):
                return value * flag_lo if e < HALO else value * flag_hi if e >= HALO + X else value

            for e in range(XE):
                value = stages[2].push(vs[c % 2, pl.ds(e * 8, 8), pl.ds(256, 128)])
                if value is None:
                    continue
                value = mask(value, e - 3) + vs[c % 2, pl.ds((e - 3) * 8, 8), pl.ds(128, 128)]
                value = stages[1].push(value)
                if value is None:
                    continue
                value = mask(value, e - 6) + vs[c % 2, pl.ds((e - 6) * 8, 8), pl.ds(0, 128)]
                value = stages[0].push(value)
                if value is None:
                    continue
                at = e - 9
                start = ut[f, c, pl.ds(at * 8, 8), :] if c < TILES else hs[pl.ds(at * 8 + 48, 8), :]
                value = mask(value, at) + 4.0 * start
                if c == TILES:
                    de[f, at - 9] = value
                else:
                    dg[2 * c, f, at - 9] = value
        for x in range(1, X + 1):
            turned = [pltpu.roll(dg[2 * c, f, x], 64, 1) for c in range(TILES)]
            for c in range(TILES - 1):
                dg[2 * c + 1, f, x] = jnp.where(low_half, turned[c], turned[c + 1])
        return carry

    lax.fori_loop(0, F, per_field, 0)

    def record_copy(k):
        offset = (lax.div(k, 3) - 1, lax.rem(k, 3) - 1)
        return remote(values_ref.at[k], arrived.at[k], record_send.at[k], record_recv.at[k], offset)

    def per_code(k, carry):
        def per_group(group, held):
            held = list(held)
            weights = [wide_ref[i, pl.ds(pl.multiple_of(k * CAP + group * 8, 8), 8), :] for i in range(4)]
            for j in range(8):
                slot = group * 8 + j
                window = info[k, 0, slot]
                start = info[k, 1, slot] + 1
                rows = [jnp.broadcast_to(weights[i][j : j + 1, :], (8, LANES)) for i in range(4)]
                for f in range(F):
                    total = dg[window, f, start] * rows[0]
                    for i in range(1, 4):
                        total = total + dg[window, f, start + i] * rows[i]
                    value = jnp.sum(total, axis=1, keepdims=True) * SIGNS[f]
                    held[f] = jnp.where(lane == slot, value, held[f])
            return tuple(held)

        held = lax.fori_loop(0, CAP // 8, per_group, tuple(jnp.zeros((8, LANES), F32) for _ in range(F)))
        for f in range(F):
            values_ref[k, pl.ds(f * 8, 8), :] = held[f]

        @pl.when(k != 4)
        def _():
            record_copy(k).start()

        return carry

    lax.fori_loop(0, 9, per_code, 0)
    own_values = pltpu.make_async_copy(values_ref.at[4], arrived.at[4], out_sems.at[1])
    own_values.start()

    mix_x = [[flux_x[f, g] * -0.125 for g in range(F)] for f in range(F)]
    mix_y = [[flux_y[f, g] * -0.125 for g in range(F)] for f in range(F)]

    def per_octet(octet, carry):
        for c in range(TILES):
            solid = solid_ref[pl.ds(pl.multiple_of(octet * 8, 8), 8), pl.ds(c * LANES, LANES)]
            for half in range(4):
                first = octet * 8 + half * 2
                here = pl.ds(first + 1, 2)
                slopes_x, slopes_y, mids = [], [], []
                wide_lane = lax.broadcasted_iota(I32, (2, 8, LANES), 2)
                for g in range(F):
                    mid = dg[2 * c, g, here]
                    before = dg[2 * c, g, pl.ds(first, 2)]
                    after = dg[2 * c, g, pl.ds(first + 2, 2)]
                    left = dg[2 * (c - 1), g, here] if c > 0 else de[g, here]
                    right = dg[2 * (c + 1), g, here] if c < TILES - 1 else de[g, here]
                    up = jnp.where(wide_lane == LANES - 1, pltpu.roll(right, LANES - 1, 2), pltpu.roll(mid, LANES - 1, 2))
                    down = jnp.where(wide_lane == 0, pltpu.roll(left, 1, 2), pltpu.roll(mid, 1, 2))
                    mids.append(mid)
                    slopes_x.append(after - before)
                    slopes_y.append(up - down)
                for f in range(F):
                    total = -0.125 * mids[f]
                    for g in range(F):
                        total = total + mix_x[f][g] * slopes_x[g] + mix_y[f][g] * slopes_y[g]
                    for i in range(2):
                        x = octet * 8 + half * 2 + i
                        cells = total[i] + 1.125 * ub[c, f, pl.ds(x, 8, stride=X), :]
                        row = half * 2 + i
                        blocked = jnp.broadcast_to(solid[row : row + 1, :], (8, LANES)) == 1
                        section_ref[c, f, pl.ds(pl.multiple_of((first + i) * 8, 8), 8), :] = jnp.where(blocked, 0.0, cells)
        return carry

    written = []
    for half in range(2):
        lax.fori_loop(half * 4, half * 4 + 4, per_octet, 0)
        rows = pl.ds(half * 256, 256)
        written.append(
            pltpu.make_async_copy(section_ref.at[:, :, rows], section_hbm.at[:, :, rows], out_sems.at[2 + half])
        )
        written[-1].start()

    def finish_field(f, carry):
        for copy in row_copies(f):
            copy.wait_send()
        return carry

    lax.fori_loop(0, F, finish_field, 0)
    for copy in side_copies:
        copy.wait_send()
    for k in range(9):
        if k != 4:
            record_copy(k).wait()
    for copy in written + [own_ghosts, own_values]:
        copy.wait()


def scatter_kernel(info, section_hbm, arrived, out_hbm, work, natural, sems):
    loading = pltpu.make_async_copy(section_hbm, work, sems.at[TILES])
    loading.start()
    gx, gy = lax.axis_index("gx"), lax.axis_index("gy")
    nx, ny = lax.axis_size("gx"), lax.axis_size("gy")
    lane = lane_index()
    loading.wait()

    def per_code(k, carry):
        from_x, from_y = gx - lax.div(k, 3) + 1, gy - lax.rem(k, 3) + 1
        weight = jnp.where((from_x >= 0) & (from_x < nx) & (from_y >= 0) & (from_y < ny), 1.0, 0.0).astype(F32)
        blocks = [arrived[k, pl.ds(f * 8, 8), :] * weight for f in range(F)]
        for j in range(CAP):
            start = pl.multiple_of(info[k, 2, j] * 8, 8)
            tile = info[k, 3, j]
            hit = lane == info[k, 4, j]
            for f in range(F):
                value = jnp.broadcast_to(blocks[f][:, j : j + 1], (8, LANES))
                rows = pl.ds(start, 8)
                work[tile, f, rows, :] = work[tile, f, rows, :] + jnp.where(hit, value, 0.0)
        return carry

    lax.fori_loop(0, 9, per_code, 0)
    copies = []
    for c in range(TILES):

        def per_field(f, carry):
            for x in range(X):
                natural[c, f, pl.ds(x, 8, stride=X), :] = work[c, f, pl.ds(x * 8, 8), :]
            return carry

        lax.fori_loop(0, F, per_field, 0)
        copy = pltpu.make_async_copy(natural.at[c], out_hbm.at[:, :, pl.ds(c * LANES, LANES)], sems.at[c])
        copy.start()
        copies.append(copy)
    for copy in copies:
        copy.wait()


def space(kind, count):
    return [pl.BlockSpec(memory_space=kind)] * count


def shards(conserved, solid_cells, flux_x, flux_y, counts, owner_offset, stencil_base, weights, ghost_cells,
           first_matrix, rest_matrix):
    shape = jax.ShapeDtypeStruct
    u = conserved.reshape(F, Z * X, Y)
    vmem, smem, anywhere = pltpu.VMEM, pltpu.SMEM, pl.ANY
    dma = pltpu.SemaphoreType.DMA
    info, wide = pl.pallas_call(
        prepare_kernel,
        out_shape=[shape((9, 8, LANES), I32), shape((4, REC, LANES), F32)],
        in_specs=space(smem, 1) + space(vmem, 4),
        out_specs=space(vmem, 2),
        compiler_params=pltpu.CompilerParams(vmem_limit_bytes=VMEM_BYTES),
        name="prepare",
    )(counts, owner_offset, stencil_base, ghost_cells, weights.T)
    section, arrived, ghosts = pl.pallas_call(
        main_kernel,
        out_shape=[
            shape((TILES, F, X * Z, LANES), F32), shape((9, F * Z, LANES), F32), shape((9, 8, LANES), I32),
        ],
        in_specs=space(smem, 3) + space(anywhere, 2) + space(vmem, 1) + space(anywhere, 2) + space(vmem, 1),
        out_specs=space(anywhere, 3),
        scratch_shapes=[
            pltpu.VMEM((TILES, F, Z * X, LANES), F32),
            pltpu.VMEM((4, 512, 128), BF16), pltpu.VMEM((4, 768, 256), BF16),
            pltpu.VMEM((F, TILES, ROWS, LANES), F32), pltpu.VMEM((768, LANES), F32),
        ] + [pltpu.VMEM((TILES + 1, ROWS, LANES), BF16)] * 4 + [
            pltpu.VMEM((2, ROWS, 384), F32),
            pltpu.VMEM((7, F, X + 2, Z, LANES), F32), pltpu.VMEM((F, X + 2, Z, LANES), F32),
            pltpu.VMEM((TILES, F, X * Z, LANES), F32), pltpu.VMEM((9, F * Z, LANES), F32),
        ] + [pltpu.VMEM((F, HALO * 8, Y), F32)] * 2 + [pltpu.VMEM((F, X, LANES), F32)] * 2
        + [pltpu.VMEM((F, HALO * 8, Y), F32)] * 2 + [pltpu.VMEM((F, X, LANES), F32)] * 2
        + [pltpu.VMEM((F, 16, LANES), F32)] * 4
        + [dma((12,)), dma((2, F)), dma((2, F)), dma((14,)), dma((14,)), dma((9,)), dma((9,)), dma((4,))],
        compiler_params=pltpu.CompilerParams(collective_id=0, has_side_effects=True, vmem_limit_bytes=VMEM_BYTES),
        name="section",
    )(flux_x, flux_y, info, u, info, solid_cells, first_matrix, rest_matrix, wide)
    out = pl.pallas_call(
        scatter_kernel,
        out_shape=shape((F, Z * X, Y), F32),
        in_specs=space(smem, 1) + space(anywhere, 1) + space(vmem, 1),
        out_specs=pl.BlockSpec(memory_space=anywhere),
        scratch_shapes=[
            pltpu.VMEM((TILES, F, X * Z, LANES), F32), pltpu.VMEM((TILES, F, Z * X, LANES), F32), dma((TILES + 1,)),
        ],
        compiler_params=pltpu.CompilerParams(vmem_limit_bytes=VMEM_BYTES),
        name="scatter",
    )(ghosts, section, arrived)
    return out.reshape(F, Z, X, Y)


def solution(mesh):
    first, rest = filter_constants()

    def advance(*arguments):
        run = jax.shard_map(
            shards,
            mesh=mesh,
            in_specs=(
                P(None, None, "gx", "gy"), P("gx", "gy"), P(), P(), P(("gx", "gy")), P(("gx", "gy")),
                P(("gx", "gy")), P(("gx", "gy"), None), P(("gx", "gy")), P(), P(),
            ),
            out_specs=P(None, None, "gx", "gy"),
            check_vma=False,
        )
        return run(*arguments, jnp.asarray(first), jnp.asarray(rest))

    return advance
```

```python
import functools

import jax
import jax.numpy as jnp
import ml_dtypes
import numpy as np
from jax import lax
from jax.experimental import pallas as pl
from jax.experimental.pallas import tpu as pltpu
from jax.sharding import PartitionSpec as P

F, Z, X, Y = 5, 8, 64, 512
LANES = 128
TILES = Y // LANES
HALO = 10
XE = X + 2 * HALO
ROWS = XE * Z
REC = 576
CAP = 64
SIGNS = (1.0, -1.0, -1.0, -1.0, 1.0)
F32, BF16, I32 = jnp.float32, jnp.bfloat16, jnp.int32
VMEM_BYTES = 60 * 1024 * 1024
OFFSETS = [(k // 3 - 1, k % 3 - 1) for k in range(9)]


def y_matrices(left_edge, right_edge):
    margin = 80
    ys = np.arange(-margin, Y + margin)
    inside = np.ones(ys.shape, bool)
    if left_edge:
        inside &= ys >= 0
    if right_edge:
        inside &= ys < Y
    taps = np.array([1, 6, 15, 20, 15, 6, 1], np.float64) / 64
    single = np.zeros((ys.size, ys.size))
    for offset in range(-3, 4):
        single += np.diag(np.full(ys.size - abs(offset), taps[offset + 3]), offset)
    single = single * inside[:, None] * inside[None, :]
    double = single @ single
    triple = double @ single
    return [-6.0 / 64 * single, 4.0 / 64**2 * double, -1.0 / 64**3 * triple], margin


def block_matrix(powers, margin, y_in, y_out):
    columns = []
    for power in powers:
        full = np.zeros((256, LANES))
        for lane, y in enumerate(y_out):
            if y is not None:
                full[:, lane] = power[y + margin, np.asarray(y_in) + margin]
        columns.append(full)
    return np.concatenate(columns, axis=1)


def filter_constants():
    lane = np.arange(LANES)
    found = []
    for kind in ("mid", "left", "right", "edge_left", "edge_mid", "edge_right"):
        powers, margin = y_matrices(kind.endswith("left"), kind.endswith("right"))
        if kind.startswith("edge"):
            y_in = np.concatenate([np.where(lane < 64, lane, 384 + lane), np.where(lane < 64, Y + lane, lane - 128)])
            y_out = [Y] + [None] * 126 + [-1]
        else:
            c = {"mid": 1, "left": 0, "right": 3}[kind]
            y_in = np.concatenate([128 * c + lane, np.where(lane < 64, 128 * (c + 1) + lane, 128 * (c - 1) + lane)])
            y_out = list(128 * c + lane)
        found.append(block_matrix(powers, margin, np.clip(y_in, -margin, Y + margin - 1), y_out))
    whole = np.stack(found).astype(np.float32)
    high = whole.astype(ml_dtypes.bfloat16)
    low = (whole - high.astype(np.float32)).astype(ml_dtypes.bfloat16)
    first = np.concatenate([high, high], axis=1)[:, :, :128]
    rest = np.concatenate([high, high, low], axis=1)[:, :, 128:]
    return first, rest


def lane_index(rows=8):
    return lax.broadcasted_iota(I32, (rows, LANES), 1)


ACROSS = (((1,), (1,)), ((), ()))


def place_records(count_ref, code_ref, base_ref):
    code = code_ref[...].reshape(1, REC)
    base = base_ref[...].reshape(1, REC)
    kinds = lax.broadcasted_iota(I32, (16, REC), 0)
    hits = (kinds == code).astype(F32)
    before = (lax.broadcasted_iota(I32, (REC, REC), 0) < lax.broadcasted_iota(I32, (REC, REC), 1)).astype(F32).astype(BF16)
    ahead = jnp.dot(hits.astype(BF16), before, preferred_element_type=F32)
    rank = jnp.sum(ahead * hits, axis=0, keepdims=True).astype(I32)
    slot = code * CAP + rank
    live = lax.broadcasted_iota(I32, (1, REC), 1) < count_ref[0]
    slot = jnp.where(live, slot, REC)
    placing = (lax.broadcasted_iota(I32, (REC, REC), 0) == slot).astype(F32).astype(BF16)
    base_x = ((base.astype(F32) + 0.5) * (1.0 / (Y - 3))).astype(I32)
    base_y = base - base_x * (Y - 3)
    window = jnp.minimum(base_y // 64, 6)
    return placing, window, base_x, base_y - window * 64


def prepare_kernel(count_ref, code_ref, base_ref, ghost_ref, info_ref):
    placing, window, base_x, _ = place_records(count_ref, code_ref, base_ref)
    ghost = ghost_ref[...].reshape(1, REC)
    ghost_y = ghost % Y
    payload_rows = [window, base_x, ghost // Y, ghost_y // LANES, ghost_y % LANES]
    row_id = lax.broadcasted_iota(I32, (8, REC), 0)
    payload = jnp.zeros((8, REC), I32)
    for row, value in enumerate(payload_rows):
        payload = jnp.where(row_id == row, value, payload)
    payload = payload.astype(F32).astype(BF16)
    for k in range(9):
        part = lax.dot_general(payload, placing[k * CAP : (k + 1) * CAP], ACROSS, preferred_element_type=F32)
        info_ref[k] = jnp.concatenate([part, jnp.zeros((8, LANES - CAP), F32)], axis=1).astype(I32)


def spread_weights(count_ref, code_ref, base_ref, weight_ref, wide_ref):
    placing, _, _, first_lane = place_records(count_ref, code_ref, base_ref)
    lanes_hit = (lax.broadcasted_iota(I32, (LANES, REC), 0) == first_lane).astype(F32).astype(BF16)
    starts = lax.dot_general(placing, lanes_hit, ACROSS, preferred_element_type=F32)
    weight = weight_ref[...]
    weight_a = weight.astype(BF16)
    left_over = weight - weight_a.astype(F32)
    weight_b = left_over.astype(BF16)
    weight_c = (left_over - weight_b.astype(F32)).astype(BF16)
    ordered = sum(
        lax.dot_general(placing, part, ACROSS, preferred_element_type=F32) for part in (weight_a, weight_b, weight_c)
    )
    shifted = [starts] + [pltpu.roll(starts, j, 1) for j in range(1, 4)]
    for i in range(4):
        total = shifted[0] * ordered[:, 4 * i : 4 * i + 1]
        for j in range(1, 4):
            total = total + shifted[j] * ordered[:, 4 * i + j : 4 * i + j + 1]
        wide_ref[i] = total


def neighbour(dx, dy):
    nx, ny = lax.axis_size("gx"), lax.axis_size("gy")
    return (lax.rem(lax.axis_index("gx") + dx + nx, nx), lax.rem(lax.axis_index("gy") + dy + ny, ny))


def signal_neighbours():
    barrier = pltpu.get_barrier_semaphore()
    for dx, dy in OFFSETS:
        if (dx, dy) != (0, 0):
            pl.semaphore_signal(barrier, inc=1, device_id=neighbour(dx, dy), device_id_type=pl.DeviceIdType.MESH)


def wait_neighbours():
    pl.semaphore_wait(pltpu.get_barrier_semaphore(), 8)


class Binomial:
    def __init__(self):
        self.held = [None] * 6

    def push(self, value):
        for i in range(6):
            before, self.held[i] = self.held[i], value
            if before is None:
                return None
            value = before + value
        return value


def remote(source, target, send_sem, recv_sem, offset):
    return pltpu.make_async_remote_copy(
        src_ref=source, dst_ref=target, send_sem=send_sem, recv_sem=recv_sem,
        device_id=neighbour(*offset), device_id_type=pl.DeviceIdType.MESH,
    )


def main_kernel(flux_x, flux_y, count_ref, info, u_hbm, info_hbm, code_ref, base_ref, weight_ref, solid_ref, first_hbm, rest_hbm,
                section_hbm, arrived, ghosts,
                ub, firsts, rests, ut, hs, hi_main, lo_main, hi_side, lo_side, vs, dg, de, section_ref, values_ref,
                low_ref, high_ref, left_ref, right_ref, xlo, xhi, ylo, yhi, cll, clr, chl, chr_,
                wide_ref, sems, row_send, row_recv, side_send, side_recv, record_send, record_recv, out_sems):
    signal_neighbours()
    gx, gy = lax.axis_index("gx"), lax.axis_index("gy")
    last_x, last_y = lax.axis_size("gx") - 1, lax.axis_size("gy") - 1
    flag_lo = jnp.where(gx > 0, 1.0, 0.0).astype(F32)
    flag_hi = jnp.where(gx < last_x, 1.0, 0.0).astype(F32)
    flag_left = jnp.where(gy > 0, 1.0, 0.0).astype(F32)
    flag_right = jnp.where(gy < last_y, 1.0, 0.0).astype(F32)
    kinds = [
        jnp.where(gy == 0, 1, 0),
        0,
        jnp.where(gy == last_y, 2, 0),
        jnp.where(gy == 0, 3, jnp.where(gy == last_y, 5, 4)),
    ]
    copies = [
        pltpu.make_async_copy(u_hbm.at[:, :, pl.ds(c * LANES, LANES)], ub.at[c], sems.at[c]) for c in range(TILES)
    ]
    constant_copies = []
    for i, kind in enumerate(kinds):
        constant_copies.append(pltpu.make_async_copy(first_hbm.at[kind], firsts.at[i], sems.at[4 + i]))
        constant_copies.append(pltpu.make_async_copy(rest_hbm.at[kind], rests.at[i], sems.at[8 + i]))
    for copy in copies + constant_copies:
        copy.start()
    for copy in copies:
        copy.wait()
    lane = lane_index()
    low_half = lane < 64

    def pack_sides(f, carry):
        for octet in range(8):
            left = jnp.zeros((8, LANES), F32)
            right = jnp.zeros((8, LANES), F32)
            for z in range(Z):
                here = (lane // 16) == z
                row = z * X + octet * 8
                left = jnp.where(here, pltpu.roll(ub[0, f, pl.ds(row, 8), :], 16 * z, 1), left)
                right = jnp.where(
                    here, pltpu.roll(ub[TILES - 1, f, pl.ds(row, 8), :], (16 * z - (LANES - HALO)) % LANES, 1), right
                )
            left_ref[f, pl.ds(octet * 8, 8), :] = left
            right_ref[f, pl.ds(octet * 8, 8), :] = right
        return carry

    lax.fori_loop(0, F, pack_sides, 0)
    wait_neighbours()
    plan = [
        (right_ref, ylo, (0, 1)),
        (left_ref, yhi, (0, -1)),
        (right_ref.at[:, pl.ds(X - 16, 16)], cll, (1, 1)),
        (left_ref.at[:, pl.ds(X - 16, 16)], clr, (1, -1)),
        (right_ref.at[:, pl.ds(0, 16)], chl, (-1, 1)),
        (left_ref.at[:, pl.ds(0, 16)], chr_, (-1, -1)),
    ]
    side_copies = [
        remote(source, target, side_send.at[index], side_recv.at[index], offset)
        for index, (source, target, offset) in enumerate(plan)
    ]
    for copy in side_copies:
        copy.start()

    def pack_rows(f, carry):
        for c in range(TILES):
            for x in range(HALO):
                low_ref[f, pl.ds(x * 8, 8), pl.ds(c * LANES, LANES)] = ub[c, f, pl.ds(x, 8, stride=X), :]
                high_ref[f, pl.ds(x * 8, 8), pl.ds(c * LANES, LANES)] = ub[c, f, pl.ds(X - HALO + x, 8, stride=X), :]
        return carry

    lax.fori_loop(0, F, pack_rows, 0)
    def row_copies(f):
        return (
            remote(high_ref.at[f], xlo.at[f], row_send.at[0, f], row_recv.at[0, f], (1, 0)),
            remote(low_ref.at[f], xhi.at[f], row_send.at[1, f], row_recv.at[1, f], (-1, 0)),
        )

    for f in range(F):
        for copy in row_copies(f):
            copy.start()

    spread_weights(count_ref, code_ref, base_ref, weight_ref, wide_ref)
    ghost_copies = [
        remote(info_hbm.at[k], ghosts.at[k], side_send.at[6 + k], side_recv.at[6 + k], offset)
        for k, offset in enumerate(OFFSETS) if k != 4
    ]
    for copy in ghost_copies:
        copy.start()
    own_ghosts = pltpu.make_async_copy(info_hbm.at[4], ghosts.at[4], out_sems.at[0])
    own_ghosts.start()

    def turn(f, carry):
        for c in range(TILES):
            for x in range(X):
                ut[f, c, pl.ds((HALO + x) * 8, 8), :] = ub[c, f, pl.ds(x, 8, stride=X), :]
        return carry

    lax.fori_loop(0, F, turn, 0)
    for copy in constant_copies:
        copy.wait()
    for copy in side_copies:
        copy.wait_recv()

    def per_field(f, carry):
        for copy in row_copies(f):
            copy.wait_recv()
        for c in range(TILES):
            ut[f, c, pl.ds(0, 80), :] = xlo[f, :, pl.ds(c * LANES, LANES)] * flag_lo
            ut[f, c, pl.ds(ROWS - 80, 80), :] = xhi[f, :, pl.ds(c * LANES, LANES)] * flag_hi
        for octet in range(-2, 10):
            if octet < 0:
                left, right = [r[f, pl.ds((octet + 2) * 8, 8), :] * flag_lo for r in (cll, clr)]
            elif octet >= 8:
                left, right = [r[f, pl.ds((octet - 8) * 8, 8), :] * flag_hi for r in (chl, chr_)]
            else:
                left, right = [r[f, pl.ds(octet * 8, 8), :] for r in (ylo, yhi)]
            left, right = left * flag_left, right * flag_right
            for z in range(Z):
                from_right = pltpu.roll(right, (-16 * z) % LANES, 1)
                from_left = pltpu.roll(left, (LANES - HALO - 16 * z) % LANES, 1)
                hs[pl.ds((octet + 2) * 64 + z, 8, stride=8), :] = jnp.where(low_half, from_right, from_left)

        keep_low = (lane_index(16) < 64).astype(F32).astype(BF16)
        keep_high = (lane_index(16) >= 64).astype(F32).astype(BF16)
        for block in range(ROWS // 16):
            rows = pl.ds(block * 16, 16)
            highs, lows = [], []
            for c in range(TILES + 1):
                value = ut[f, c, rows, :] if c < TILES else hs[pl.ds(block * 16 + 48, 16), :]
                high = value.astype(BF16)
                low = (value - high.astype(F32)).astype(BF16)
                highs.append(high)
                lows.append(low)
            for parts, main, side in ((highs, hi_main, hi_side), (lows, lo_main, lo_side)):
                lo_parts = [p * keep_low for p in parts]
                hi_parts = [p * keep_high for p in parts]
                for c in range(TILES):
                    main[c, rows, :] = parts[c]
                    after = lo_parts[c + 1] if c < TILES - 1 else lo_parts[TILES]
                    ahead = hi_parts[c - 1] if c > 0 else hi_parts[TILES]
                    side[c, rows, :] = after + ahead
                main[TILES, rows, :] = lo_parts[0] + hi_parts[TILES - 1]
                side[TILES, rows, :] = parts[TILES]

        for c in range(TILES + 1):
            which = (0, 1, 1, 2, 3)[c]
            high = jnp.concatenate([hi_main[c], hi_side[c]], axis=1)
            low = jnp.concatenate([lo_main[c], lo_side[c]], axis=1)
            vs[c % 2, :, pl.ds(0, 128)] = jnp.dot(
                jnp.concatenate([high, low], axis=1), firsts[which], preferred_element_type=F32
            )
            vs[c % 2, :, pl.ds(128, 256)] = jnp.dot(
                jnp.concatenate([high, low, high], axis=1), rests[which], preferred_element_type=F32
            )
            stages = [Binomial(), Binomial(), Binomial()]

            def mask(value, e):
                return value * flag_lo if e < HALO else value * flag_hi if e >= HALO + X else value

            for e in range(XE):
                value = stages[2].push(vs[c % 2, pl.ds(e * 8, 8), pl.ds(256, 128)])
                if value is None:
                    continue
                value = mask(value, e - 3) + vs[c % 2, pl.ds((e - 3) * 8, 8), pl.ds(128, 128)]
                value = stages[1].push(value)
                if value is None:
                    continue
                value = mask(value, e - 6) + vs[c % 2, pl.ds((e - 6) * 8, 8), pl.ds(0, 128)]
                value = stages[0].push(value)
                if value is None:
                    continue
                at = e - 9
                start = ut[f, c, pl.ds(at * 8, 8), :] if c < TILES else hs[pl.ds(at * 8 + 48, 8), :]
                value = mask(value, at) + 4.0 * start
                if c == TILES:
                    de[f, at - 9] = value
                else:
                    dg[2 * c, f, at - 9] = value
        for x in range(1, X + 1):
            turned = [pltpu.roll(dg[2 * c, f, x], 64, 1) for c in range(TILES)]
            for c in range(TILES - 1):
                dg[2 * c + 1, f, x] = jnp.where(low_half, turned[c], turned[c + 1])
        return carry

    lax.fori_loop(0, F, per_field, 0)

    def record_copy(k):
        offset = (lax.div(k, 3) - 1, lax.rem(k, 3) - 1)
        return remote(values_ref.at[k], arrived.at[k], record_send.at[k], record_recv.at[k], offset)

    def per_code(k, carry):
        held = [jnp.zeros((8, LANES), F32) for _ in range(F)]
        for group in range(CAP // 8):
            weights = [wide_ref[i, pl.ds(pl.multiple_of(k * CAP + group * 8, 8), 8), :] for i in range(4)]
            for j in range(8):
                slot = group * 8 + j
                window = info[k, 0, slot]
                start = info[k, 1, slot] + 1
                rows = [jnp.broadcast_to(weights[i][j : j + 1, :], (8, LANES)) for i in range(4)]
                for f in range(F):
                    total = dg[window, f, start] * rows[0]
                    for i in range(1, 4):
                        total = total + dg[window, f, start + i] * rows[i]
                    value = jnp.sum(total, axis=1, keepdims=True) * SIGNS[f]
                    held[f] = jnp.where(lane == slot, value, held[f])
        for f in range(F):
            values_ref[k, pl.ds(f * 8, 8), :] = held[f]

        @pl.when(k != 4)
        def _():
            record_copy(k).start()

        return carry

    lax.fori_loop(0, 9, per_code, 0)
    own_values = pltpu.make_async_copy(values_ref.at[4], arrived.at[4], out_sems.at[1])
    own_values.start()

    mix_x = [[flux_x[f, g] * -0.125 for g in range(F)] for f in range(F)]
    mix_y = [[flux_y[f, g] * -0.125 for g in range(F)] for f in range(F)]

    def per_octet(octet, carry):
        for c in range(TILES):
            solid = solid_ref[pl.ds(pl.multiple_of(octet * 8, 8), 8), pl.ds(c * LANES, LANES)]
            for half in range(4):
                first = octet * 8 + half * 2
                here = pl.ds(first + 1, 2)
                slopes_x, slopes_y, mids = [], [], []
                wide_lane = lax.broadcasted_iota(I32, (2, 8, LANES), 2)
                for g in range(F):
                    mid = dg[2 * c, g, here]
                    before = dg[2 * c, g, pl.ds(first, 2)]
                    after = dg[2 * c, g, pl.ds(first + 2, 2)]
                    left = dg[2 * (c - 1), g, here] if c > 0 else de[g, here]
                    right = dg[2 * (c + 1), g, here] if c < TILES - 1 else de[g, here]
                    up = jnp.where(wide_lane == LANES - 1, pltpu.roll(right, LANES - 1, 2), pltpu.roll(mid, LANES - 1, 2))
                    down = jnp.where(wide_lane == 0, pltpu.roll(left, 1, 2), pltpu.roll(mid, 1, 2))
                    mids.append(mid)
                    slopes_x.append(after - before)
                    slopes_y.append(up - down)
                for f in range(F):
                    total = -0.125 * mids[f]
                    for g in range(F):
                        total = total + mix_x[f][g] * slopes_x[g] + mix_y[f][g] * slopes_y[g]
                    for i in range(2):
                        x = octet * 8 + half * 2 + i
                        cells = total[i] + 1.125 * ut[f, c, pl.ds(pl.multiple_of((x + HALO) * 8, 8), 8), :]
                        row = half * 2 + i
                        blocked = jnp.broadcast_to(solid[row : row + 1, :], (8, LANES)) == 1
                        section_ref[c, f, pl.ds(pl.multiple_of((first + i) * 8, 8), 8), :] = jnp.where(blocked, 0.0, cells)
        return carry

    written = []
    for half in range(2):
        lax.fori_loop(half * 4, half * 4 + 4, per_octet, 0)
        rows = pl.ds(half * 256, 256)
        written.append(
            pltpu.make_async_copy(section_ref.at[:, :, rows], section_hbm.at[:, :, rows], out_sems.at[2 + half])
        )
        written[-1].start()

    def finish_field(f, carry):
        for copy in row_copies(f):
            copy.wait_send()
        return carry

    lax.fori_loop(0, F, finish_field, 0)
    for copy in side_copies:
        copy.wait_send()
    for copy in ghost_copies:
        copy.wait()
    for k in range(9):
        if k != 4:
            record_copy(k).wait()
    for copy in written + [own_ghosts, own_values]:
        copy.wait()


def scatter_kernel(info, section_hbm, arrived, out_hbm, section_ref, work, natural, sems):
    loading = pltpu.make_async_copy(section_hbm, section_ref, sems.at[TILES])
    loading.start()
    gx, gy = lax.axis_index("gx"), lax.axis_index("gy")
    nx, ny = lax.axis_size("gx"), lax.axis_size("gy")
    lane = lane_index()

    def clear(f, carry):
        for c in range(TILES):
            for x in range(X):
                work[c, f, pl.ds(x * 8, 8), :] = jnp.zeros((8, LANES), F32)
        return carry

    lax.fori_loop(0, F, clear, 0)

    def per_code(k, carry):
        from_x, from_y = gx - lax.div(k, 3) + 1, gy - lax.rem(k, 3) + 1
        weight = jnp.where((from_x >= 0) & (from_x < nx) & (from_y >= 0) & (from_y < ny), 1.0, 0.0).astype(F32)
        blocks = [arrived[k, pl.ds(f * 8, 8), :] * weight for f in range(F)]
        for j in range(CAP):
            start = pl.multiple_of(info[k, 2, j] * 8, 8)
            tile = info[k, 3, j]
            hit = lane == info[k, 4, j]
            rows = pl.ds(start, 8)
            held = [work[tile, f, rows, :] for f in range(F)]
            for f in range(F):
                value = jnp.broadcast_to(blocks[f][:, j : j + 1], (8, LANES))
                held[f] = held[f] + jnp.where(hit, value, 0.0)
            for f in range(F):
                work[tile, f, rows, :] = held[f]
        return carry

    lax.fori_loop(0, 9, per_code, 0)
    loading.wait()
    copies = []
    for c in range(TILES):

        def per_field(f, carry):
            for x in range(X):
                rows = pl.ds(x * 8, 8)
                natural[c, f, pl.ds(x, 8, stride=X), :] = section_ref[c, f, rows, :] + work[c, f, rows, :]
            return carry

        lax.fori_loop(0, F, per_field, 0)
        copy = pltpu.make_async_copy(natural.at[c], out_hbm.at[:, :, pl.ds(c * LANES, LANES)], sems.at[c])
        copy.start()
        copies.append(copy)
    for copy in copies:
        copy.wait()


def space(kind, count):
    return [pl.BlockSpec(memory_space=kind)] * count


def shards(conserved, solid_cells, flux_x, flux_y, counts, owner_offset, stencil_base, weights, ghost_cells,
           first_matrix, rest_matrix):
    shape = jax.ShapeDtypeStruct
    u = conserved.reshape(F, Z * X, Y)
    vmem, smem, anywhere = pltpu.VMEM, pltpu.SMEM, pl.ANY
    dma = pltpu.SemaphoreType.DMA
    info = pl.pallas_call(
        prepare_kernel,
        out_shape=shape((9, 8, LANES), I32),
        in_specs=space(smem, 1) + space(vmem, 3),
        out_specs=pl.BlockSpec(memory_space=vmem),
        compiler_params=pltpu.CompilerParams(vmem_limit_bytes=VMEM_BYTES),
        name="prepare",
    )(counts, owner_offset, stencil_base, ghost_cells)
    section, arrived, ghosts = pl.pallas_call(
        main_kernel,
        out_shape=[
            shape((TILES, F, X * Z, LANES), F32), shape((9, F * Z, LANES), F32), shape((9, 8, LANES), I32),
        ],
        in_specs=space(smem, 4) + space(anywhere, 2) + space(vmem, 4) + space(anywhere, 2),
        out_specs=space(anywhere, 3),
        scratch_shapes=[
            pltpu.VMEM((TILES, F, Z * X, LANES), F32),
            pltpu.VMEM((4, 512, 128), BF16), pltpu.VMEM((4, 768, 256), BF16),
            pltpu.VMEM((F, TILES, ROWS, LANES), F32), pltpu.VMEM((768, LANES), F32),
        ] + [pltpu.VMEM((TILES + 1, ROWS, LANES), BF16)] * 4 + [
            pltpu.VMEM((2, ROWS, 384), F32),
            pltpu.VMEM((7, F, X + 2, Z, LANES), F32), pltpu.VMEM((F, X + 2, Z, LANES), F32),
            pltpu.VMEM((TILES, F, X * Z, LANES), F32), pltpu.VMEM((9, F * Z, LANES), F32),
        ] + [pltpu.VMEM((F, HALO * 8, Y), F32)] * 2 + [pltpu.VMEM((F, X, LANES), F32)] * 2
        + [pltpu.VMEM((F, HALO * 8, Y), F32)] * 2 + [pltpu.VMEM((F, X, LANES), F32)] * 2
        + [pltpu.VMEM((F, 16, LANES), F32)] * 4
        + [pltpu.VMEM((4, REC, LANES), F32)]
        + [dma((12,)), dma((2, F)), dma((2, F)), dma((15,)), dma((15,)), dma((9,)), dma((9,)), dma((4,))],
        compiler_params=pltpu.CompilerParams(collective_id=0, has_side_effects=True, vmem_limit_bytes=VMEM_BYTES),
        name="section",
    )(
        flux_x, flux_y, counts, info, u, info, owner_offset, stencil_base, weights.T, solid_cells, first_matrix, rest_matrix
    )
    out = pl.pallas_call(
        scatter_kernel,
        out_shape=shape((F, Z * X, Y), F32),
        in_specs=space(smem, 1) + space(anywhere, 1) + space(vmem, 1),
        out_specs=pl.BlockSpec(memory_space=anywhere),
        scratch_shapes=[
            pltpu.VMEM((TILES, F, X * Z, LANES), F32), pltpu.VMEM((TILES, F, X * Z, LANES), F32),
            pltpu.VMEM((TILES, F, Z * X, LANES), F32), dma((TILES + 1,)),
        ],
        compiler_params=pltpu.CompilerParams(vmem_limit_bytes=VMEM_BYTES),
        name="scatter",
    )(ghosts, section, arrived)
    return out.reshape(F, Z, X, Y)


def solution(mesh):
    first, rest = filter_constants()

    def advance(*arguments):
        run = jax.shard_map(
            shards,
            mesh=mesh,
            in_specs=(
                P(None, None, "gx", "gy"), P("gx", "gy"), P(), P(), P(("gx", "gy")), P(("gx", "gy")),
                P(("gx", "gy")), P(("gx", "gy"), None), P(("gx", "gy")), P(), P(),
            ),
            out_specs=P(None, None, "gx", "gy"),
            check_vma=False,
        )
        return run(*arguments, jnp.asarray(first), jnp.asarray(rest))

    return advance
```

```python
import functools

import jax
import jax.numpy as jnp
import ml_dtypes
import numpy as np
from jax import lax
from jax.experimental import pallas as pl
from jax.experimental.pallas import tpu as pltpu
from jax.sharding import PartitionSpec as P

F, Z, X, Y = 5, 8, 64, 512
LANES = 128
TILES = Y // LANES
HALO = 10
EDGE = 24
XE = X + 2 * HALO
ROWS = XE * Z
REC = 576
CAP = 64
SIGNS = (1.0, -1.0, -1.0, -1.0, 1.0)
F32, BF16, I32 = jnp.float32, jnp.bfloat16, jnp.int32
VMEM_BYTES = 60 * 1024 * 1024
OFFSETS = [(k // 3 - 1, k % 3 - 1) for k in range(9)]


def y_matrices(left_edge, right_edge):
    margin = 80
    ys = np.arange(-margin, Y + margin)
    inside = np.ones(ys.shape, bool)
    if left_edge:
        inside &= ys >= 0
    if right_edge:
        inside &= ys < Y
    taps = np.array([1, 6, 15, 20, 15, 6, 1], np.float64) / 64
    single = np.zeros((ys.size, ys.size))
    for offset in range(-3, 4):
        single += np.diag(np.full(ys.size - abs(offset), taps[offset + 3]), offset)
    single = single * inside[:, None] * inside[None, :]
    double = single @ single
    triple = double @ single
    return [-6.0 / 64 * single, 4.0 / 64**2 * double, -1.0 / 64**3 * triple], margin


def block_matrix(powers, margin, y_in, y_out):
    columns = []
    for power in powers:
        full = np.zeros((256, LANES))
        for lane, y in enumerate(y_out):
            if y is not None:
                full[:, lane] = power[y + margin, np.asarray(y_in) + margin]
        columns.append(full)
    return np.concatenate(columns, axis=1)


def filter_constants():
    lane = np.arange(LANES)
    found = []
    for kind in ("mid", "left", "right", "edge_left", "edge_mid", "edge_right"):
        powers, margin = y_matrices(kind.endswith("left"), kind.endswith("right"))
        if kind.startswith("edge"):
            y_in = np.concatenate([np.where(lane < 64, lane, 384 + lane), np.where(lane < 64, Y + lane, lane - 128)])
            y_out = [Y] + [None] * 126 + [-1]
        else:
            c = {"mid": 1, "left": 0, "right": 3}[kind]
            y_in = np.concatenate([128 * c + lane, np.where(lane < 64, 128 * (c + 1) + lane, 128 * (c - 1) + lane)])
            y_out = list(128 * c + lane)
        block = block_matrix(powers, margin, np.clip(y_in, -margin, Y + margin - 1), y_out)
        if kind.startswith("edge"):
            apart = block.reshape(2, LANES, 3, LANES)
            block = sum(np.roll(apart, (EDGE * f, EDGE * f), (1, 3)) for f in range(F)).reshape(256, 3 * LANES)
        found.append(block)
    whole = np.stack(found).astype(np.float32)
    high = whole.astype(ml_dtypes.bfloat16)
    low = (whole - high.astype(np.float32)).astype(ml_dtypes.bfloat16)
    first = np.concatenate([high, high], axis=1)[:, :, :128]
    rest = np.concatenate([high, high, low], axis=1)[:, :, 128:]
    return first, rest


def lane_index(rows=8):
    return lax.broadcasted_iota(I32, (rows, LANES), 1)


ACROSS = (((1,), (1,)), ((), ()))


def place_records(count_ref, code_ref, base_ref):
    code = code_ref[...].reshape(1, REC)
    base = base_ref[...].reshape(1, REC)
    kinds = lax.broadcasted_iota(I32, (16, REC), 0)
    hits = (kinds == code).astype(F32)
    before = (lax.broadcasted_iota(I32, (REC, REC), 0) < lax.broadcasted_iota(I32, (REC, REC), 1)).astype(F32).astype(BF16)
    ahead = jnp.dot(hits.astype(BF16), before, preferred_element_type=F32)
    rank = jnp.sum(ahead * hits, axis=0, keepdims=True).astype(I32)
    slot = code * CAP + rank
    live = lax.broadcasted_iota(I32, (1, REC), 1) < count_ref[0]
    slot = jnp.where(live, slot, REC)
    placing = (lax.broadcasted_iota(I32, (REC, REC), 0) == slot).astype(F32).astype(BF16)
    base_x = ((base.astype(F32) + 0.5) * (1.0 / (Y - 3))).astype(I32)
    base_y = base - base_x * (Y - 3)
    window = jnp.minimum(base_y // 64, 6)
    return placing, window, base_x, base_y - window * 64


def prepare_kernel(count_ref, code_ref, base_ref, ghost_ref, info_ref):
    placing, window, base_x, _ = place_records(count_ref, code_ref, base_ref)
    ghost = ghost_ref[...].reshape(1, REC)
    ghost_y = ghost % Y
    payload_rows = [window, base_x, ghost // Y, ghost_y // LANES, ghost_y % LANES]
    row_id = lax.broadcasted_iota(I32, (8, REC), 0)
    payload = jnp.zeros((8, REC), I32)
    for row, value in enumerate(payload_rows):
        payload = jnp.where(row_id == row, value, payload)
    payload = payload.astype(F32).astype(BF16)
    for k in range(9):
        part = lax.dot_general(payload, placing[k * CAP : (k + 1) * CAP], ACROSS, preferred_element_type=F32)
        info_ref[k] = jnp.concatenate([part, jnp.zeros((8, LANES - CAP), F32)], axis=1).astype(I32)


def spread_weights(count_ref, code_ref, base_ref, weight_ref, wide_ref):
    placing, _, _, first_lane = place_records(count_ref, code_ref, base_ref)
    lanes_hit = (lax.broadcasted_iota(I32, (LANES, REC), 0) == first_lane).astype(F32).astype(BF16)
    starts = lax.dot_general(placing, lanes_hit, ACROSS, preferred_element_type=F32)
    weight = weight_ref[...]
    weight_a = weight.astype(BF16)
    left_over = weight - weight_a.astype(F32)
    weight_b = left_over.astype(BF16)
    weight_c = (left_over - weight_b.astype(F32)).astype(BF16)
    ordered = sum(
        lax.dot_general(placing, part, ACROSS, preferred_element_type=F32) for part in (weight_a, weight_b, weight_c)
    )
    shifted = [starts] + [pltpu.roll(starts, j, 1) for j in range(1, 4)]
    for i in range(4):
        total = shifted[0] * ordered[:, 4 * i : 4 * i + 1]
        for j in range(1, 4):
            total = total + shifted[j] * ordered[:, 4 * i + j : 4 * i + j + 1]
        wide_ref[i] = total


def neighbour(dx, dy):
    nx, ny = lax.axis_size("gx"), lax.axis_size("gy")
    return (lax.rem(lax.axis_index("gx") + dx + nx, nx), lax.rem(lax.axis_index("gy") + dy + ny, ny))


def signal_neighbours():
    barrier = pltpu.get_barrier_semaphore()
    for dx, dy in OFFSETS:
        if (dx, dy) != (0, 0):
            pl.semaphore_signal(barrier, inc=1, device_id=neighbour(dx, dy), device_id_type=pl.DeviceIdType.MESH)


def wait_neighbours():
    pl.semaphore_wait(pltpu.get_barrier_semaphore(), 8)


class Binomial:
    def __init__(self):
        self.held = [None] * 6

    def push(self, value):
        for i in range(6):
            before, self.held[i] = self.held[i], value
            if before is None:
                return None
            value = before + value
        return value


def remote(source, target, send_sem, recv_sem, offset):
    return pltpu.make_async_remote_copy(
        src_ref=source, dst_ref=target, send_sem=send_sem, recv_sem=recv_sem,
        device_id=neighbour(*offset), device_id_type=pl.DeviceIdType.MESH,
    )


def main_kernel(flux_x, flux_y, count_ref, info, u_hbm, info_hbm, code_ref, base_ref, weight_ref, solid_ref, first_hbm, rest_hbm,
                section_hbm, arrived, ghosts,
                ub, firsts, rests, ut, hs, edge_in, edge_out, hi_main, lo_main, hi_side, lo_side, vs, dg, de, section_ref, values_ref,
                low_ref, high_ref, left_ref, right_ref, xlo, xhi, ylo, yhi, cll, clr, chl, chr_,
                wide_ref, sems, row_send, row_recv, side_send, side_recv, record_send, record_recv, out_sems):
    signal_neighbours()
    gx, gy = lax.axis_index("gx"), lax.axis_index("gy")
    last_x, last_y = lax.axis_size("gx") - 1, lax.axis_size("gy") - 1
    flag_lo = jnp.where(gx > 0, 1.0, 0.0).astype(F32)
    flag_hi = jnp.where(gx < last_x, 1.0, 0.0).astype(F32)
    flag_left = jnp.where(gy > 0, 1.0, 0.0).astype(F32)
    flag_right = jnp.where(gy < last_y, 1.0, 0.0).astype(F32)
    kinds = [
        jnp.where(gy == 0, 1, 0),
        0,
        jnp.where(gy == last_y, 2, 0),
        jnp.where(gy == 0, 3, jnp.where(gy == last_y, 5, 4)),
    ]
    copies = [
        pltpu.make_async_copy(u_hbm.at[:, :, pl.ds(c * LANES, LANES)], ub.at[c], sems.at[c]) for c in range(TILES)
    ]
    constant_copies = []
    for i, kind in enumerate(kinds):
        constant_copies.append(pltpu.make_async_copy(first_hbm.at[kind], firsts.at[i], sems.at[4 + i]))
        constant_copies.append(pltpu.make_async_copy(rest_hbm.at[kind], rests.at[i], sems.at[8 + i]))
    for copy in copies + constant_copies:
        copy.start()
    for copy in copies:
        copy.wait()
    lane = lane_index()
    low_half = lane < 64

    def pack_sides(f, carry):
        for octet in range(8):
            left = jnp.zeros((8, LANES), F32)
            right = jnp.zeros((8, LANES), F32)
            for z in range(Z):
                here = (lane // 16) == z
                row = z * X + octet * 8
                left = jnp.where(here, pltpu.roll(ub[0, f, pl.ds(row, 8), :], 16 * z, 1), left)
                right = jnp.where(
                    here, pltpu.roll(ub[TILES - 1, f, pl.ds(row, 8), :], (16 * z - (LANES - HALO)) % LANES, 1), right
                )
            left_ref[f, pl.ds(octet * 8, 8), :] = left
            right_ref[f, pl.ds(octet * 8, 8), :] = right
        return carry

    lax.fori_loop(0, F, pack_sides, 0)
    wait_neighbours()
    plan = [
        (right_ref, ylo, (0, 1)),
        (left_ref, yhi, (0, -1)),
        (right_ref.at[:, pl.ds(X - 16, 16)], cll, (1, 1)),
        (left_ref.at[:, pl.ds(X - 16, 16)], clr, (1, -1)),
        (right_ref.at[:, pl.ds(0, 16)], chl, (-1, 1)),
        (left_ref.at[:, pl.ds(0, 16)], chr_, (-1, -1)),
    ]
    side_copies = [
        remote(source, target, side_send.at[index], side_recv.at[index], offset)
        for index, (source, target, offset) in enumerate(plan)
    ]
    for copy in side_copies:
        copy.start()

    def pack_rows(f, carry):
        for c in range(TILES):
            for x in range(HALO):
                low_ref[f, pl.ds(x * 8, 8), pl.ds(c * LANES, LANES)] = ub[c, f, pl.ds(x, 8, stride=X), :]
                high_ref[f, pl.ds(x * 8, 8), pl.ds(c * LANES, LANES)] = ub[c, f, pl.ds(X - HALO + x, 8, stride=X), :]
        return carry

    lax.fori_loop(0, F, pack_rows, 0)
    def row_copies(f):
        return (
            remote(high_ref.at[f], xlo.at[f], row_send.at[0, f], row_recv.at[0, f], (1, 0)),
            remote(low_ref.at[f], xhi.at[f], row_send.at[1, f], row_recv.at[1, f], (-1, 0)),
        )

    for f in range(F):
        for copy in row_copies(f):
            copy.start()

    spread_weights(count_ref, code_ref, base_ref, weight_ref, wide_ref)
    ghost_copies = [
        remote(info_hbm.at[k], ghosts.at[k], side_send.at[6 + k], side_recv.at[6 + k], offset)
        for k, offset in enumerate(OFFSETS) if k != 4
    ]
    for copy in ghost_copies:
        copy.start()
    own_ghosts = pltpu.make_async_copy(info_hbm.at[4], ghosts.at[4], out_sems.at[0])
    own_ghosts.start()

    def turn(f, carry):
        for c in range(TILES):
            for x in range(X):
                ut[f, c, pl.ds((HALO + x) * 8, 8), :] = ub[c, f, pl.ds(x, 8, stride=X), :]
        return carry

    lax.fori_loop(0, F, turn, 0)
    for copy in constant_copies:
        copy.wait()
    for copy in side_copies:
        copy.wait_recv()

    def filter_block(c, which, f):
        high = jnp.concatenate([hi_main[c], hi_side[c]], axis=1)
        low = jnp.concatenate([lo_main[c], lo_side[c]], axis=1)
        vs[c % 2, :, pl.ds(0, 128)] = jnp.dot(
            jnp.concatenate([high, low], axis=1), firsts[which], preferred_element_type=F32
        )
        vs[c % 2, :, pl.ds(128, 256)] = jnp.dot(
            jnp.concatenate([high, low, high], axis=1), rests[which], preferred_element_type=F32
        )
        stages = [Binomial(), Binomial(), Binomial()]

        def mask(value, e):
            return value * flag_lo if e < HALO else value * flag_hi if e >= HALO + X else value

        for e in range(XE):
            value = stages[2].push(vs[c % 2, pl.ds(e * 8, 8), pl.ds(256, 128)])
            if value is None:
                continue
            value = mask(value, e - 3) + vs[c % 2, pl.ds((e - 3) * 8, 8), pl.ds(128, 128)]
            value = stages[1].push(value)
            if value is None:
                continue
            value = mask(value, e - 6) + vs[c % 2, pl.ds((e - 6) * 8, 8), pl.ds(0, 128)]
            value = stages[0].push(value)
            if value is None:
                continue
            at = e - 9
            start = ut[f, c, pl.ds(at * 8, 8), :] if c < TILES else edge_out[pl.ds(at * 8, 8), :]
            value = mask(value, at) + 4.0 * start
            if c == TILES:
                de[at - 9] = value
            else:
                dg[2 * c, f, at - 9] = value

    def clear_edges(e, carry):
        rows = pl.ds(pl.multiple_of(e * 8, 8), 8)
        edge_in[rows, :] = jnp.zeros((8, LANES), F32)
        edge_out[rows, :] = jnp.zeros((8, LANES), F32)
        return carry

    lax.fori_loop(0, XE, clear_edges, 0)

    def per_field(f, carry):
        for copy in row_copies(f):
            copy.wait_recv()
        for c in range(TILES):
            ut[f, c, pl.ds(0, 80), :] = xlo[f, :, pl.ds(c * LANES, LANES)] * flag_lo
            ut[f, c, pl.ds(ROWS - 80, 80), :] = xhi[f, :, pl.ds(c * LANES, LANES)] * flag_hi
        for octet in range(-2, 10):
            if octet < 0:
                left, right = [r[f, pl.ds((octet + 2) * 8, 8), :] * flag_lo for r in (cll, clr)]
            elif octet >= 8:
                left, right = [r[f, pl.ds((octet - 8) * 8, 8), :] * flag_hi for r in (chl, chr_)]
            else:
                left, right = [r[f, pl.ds(octet * 8, 8), :] for r in (ylo, yhi)]
            left, right = left * flag_left, right * flag_right
            for z in range(Z):
                from_right = pltpu.roll(right, (-16 * z) % LANES, 1)
                from_left = pltpu.roll(left, (LANES - HALO - 16 * z) % LANES, 1)
                hs[pl.ds((octet + 2) * 64 + z, 8, stride=8), :] = jnp.where(low_half, from_right, from_left)

        window = ((lane - EDGE * f + EDGE // 2) & (LANES - 1)) < EDGE
        for e in range(XE):
            rows = pl.ds(e * 8, 8)
            inner = jnp.where(low_half, ut[f, 0, rows, :], ut[f, TILES - 1, rows, :])
            edge_in[rows, :] = jnp.where(window, pltpu.roll(inner, EDGE * f, 1), edge_in[rows, :])
            outer = hs[pl.ds(e * 8 + 48, 8), :]
            edge_out[rows, :] = jnp.where(window, pltpu.roll(outer, EDGE * f, 1), edge_out[rows, :])

        keep_low = (lane_index(16) < 64).astype(F32).astype(BF16)
        keep_high = (lane_index(16) >= 64).astype(F32).astype(BF16)
        for block in range(ROWS // 16):
            rows = pl.ds(block * 16, 16)
            highs, lows = [], []
            for c in range(TILES + 1):
                value = ut[f, c, rows, :] if c < TILES else hs[pl.ds(block * 16 + 48, 16), :]
                high = value.astype(BF16)
                low = (value - high.astype(F32)).astype(BF16)
                highs.append(high)
                lows.append(low)
            for parts, main, side in ((highs, hi_main, hi_side), (lows, lo_main, lo_side)):
                lo_parts = [p * keep_low for p in parts]
                hi_parts = [p * keep_high for p in parts]
                for c in range(TILES):
                    main[c, rows, :] = parts[c]
                    after = lo_parts[c + 1] if c < TILES - 1 else lo_parts[TILES]
                    ahead = hi_parts[c - 1] if c > 0 else hi_parts[TILES]
                    side[c, rows, :] = after + ahead

        for c in range(TILES):
            filter_block(c, (0, 1, 1, 2)[c], f)
        for x in range(1, X + 1):
            turned = [pltpu.roll(dg[2 * c, f, x], 64, 1) for c in range(TILES)]
            for c in range(TILES - 1):
                dg[2 * c + 1, f, x] = jnp.where(low_half, turned[c], turned[c + 1])
        return carry

    lax.fori_loop(0, F, per_field, 0)
    for block in range(ROWS // 16):
        rows = pl.ds(block * 16, 16)
        for source, high_ref_, low_ref_ in ((edge_in, hi_main, lo_main), (edge_out, hi_side, lo_side)):
            high = source[rows, :].astype(BF16)
            high_ref_[TILES, rows, :] = high
            low_ref_[TILES, rows, :] = (source[rows, :] - high.astype(F32)).astype(BF16)
    filter_block(TILES, 3, 0)

    def record_copy(k):
        offset = (lax.div(k, 3) - 1, lax.rem(k, 3) - 1)
        return remote(values_ref.at[k], arrived.at[k], record_send.at[k], record_recv.at[k], offset)

    def per_code(k, carry):
        held = [jnp.zeros((8, LANES), F32) for _ in range(F)]
        for group in range(CAP // 8):
            weights = [wide_ref[i, pl.ds(pl.multiple_of(k * CAP + group * 8, 8), 8), :] for i in range(4)]
            for j in range(8):
                slot = group * 8 + j
                window = info[k, 0, slot]
                start = info[k, 1, slot] + 1
                rows = [jnp.broadcast_to(weights[i][j : j + 1, :], (8, LANES)) for i in range(4)]
                for f in range(F):
                    total = dg[window, f, start] * rows[0]
                    for i in range(1, 4):
                        total = total + dg[window, f, start + i] * rows[i]
                    value = jnp.sum(total, axis=1, keepdims=True) * SIGNS[f]
                    held[f] = jnp.where(lane == slot, value, held[f])
        for f in range(F):
            values_ref[k, pl.ds(f * 8, 8), :] = held[f]

        @pl.when(k != 4)
        def _():
            record_copy(k).start()

        return carry

    lax.fori_loop(0, 9, per_code, 0)
    own_values = pltpu.make_async_copy(values_ref.at[4], arrived.at[4], out_sems.at[1])
    own_values.start()

    mix_x = [[flux_x[f, g] * -0.125 for g in range(F)] for f in range(F)]
    mix_y = [[flux_y[f, g] * -0.125 for g in range(F)] for f in range(F)]

    def per_octet(octet, carry):
        for c in range(TILES):
            solid = solid_ref[pl.ds(pl.multiple_of(octet * 8, 8), 8), pl.ds(c * LANES, LANES)]
            for half in range(4):
                first = octet * 8 + half * 2
                here = pl.ds(first + 1, 2)
                slopes_x, slopes_y, mids = [], [], []
                wide_lane = lax.broadcasted_iota(I32, (2, 8, LANES), 2)
                for g in range(F):
                    mid = dg[2 * c, g, here]
                    before = dg[2 * c, g, pl.ds(first, 2)]
                    after = dg[2 * c, g, pl.ds(first + 2, 2)]
                    left = dg[2 * (c - 1), g, here] if c > 0 else de[here]
                    right = dg[2 * (c + 1), g, here] if c < TILES - 1 else de[here]
                    left_turn = 1 if c > 0 else (1 - EDGE * g) % LANES
                    right_turn = LANES - 1 if c < TILES - 1 else (LANES - 1 - EDGE * g) % LANES
                    up = jnp.where(wide_lane == LANES - 1, pltpu.roll(right, right_turn, 2), pltpu.roll(mid, LANES - 1, 2))
                    down = jnp.where(wide_lane == 0, pltpu.roll(left, left_turn, 2), pltpu.roll(mid, 1, 2))
                    mids.append(mid)
                    slopes_x.append(after - before)
                    slopes_y.append(up - down)
                for f in range(F):
                    total = -0.125 * mids[f]
                    for g in range(F):
                        total = total + mix_x[f][g] * slopes_x[g] + mix_y[f][g] * slopes_y[g]
                    for i in range(2):
                        x = octet * 8 + half * 2 + i
                        cells = total[i] + 1.125 * ut[f, c, pl.ds(pl.multiple_of((x + HALO) * 8, 8), 8), :]
                        row = half * 2 + i
                        blocked = jnp.broadcast_to(solid[row : row + 1, :], (8, LANES)) == 1
                        section_ref[c, f, pl.ds(pl.multiple_of((first + i) * 8, 8), 8), :] = jnp.where(blocked, 0.0, cells)
        return carry

    written = []
    for half in range(2):
        lax.fori_loop(half * 4, half * 4 + 4, per_octet, 0)
        rows = pl.ds(half * 256, 256)
        written.append(
            pltpu.make_async_copy(section_ref.at[:, :, rows], section_hbm.at[:, :, rows], out_sems.at[2 + half])
        )
        written[-1].start()

    def finish_field(f, carry):
        for copy in row_copies(f):
            copy.wait_send()
        return carry

    lax.fori_loop(0, F, finish_field, 0)
    for copy in side_copies:
        copy.wait_send()
    for copy in ghost_copies:
        copy.wait()
    for k in range(9):
        if k != 4:
            record_copy(k).wait()
    for copy in written + [own_ghosts, own_values]:
        copy.wait()


def scatter_kernel(info, section_hbm, arrived, out_hbm, section_ref, work, natural, sems):
    loading = pltpu.make_async_copy(section_hbm, section_ref, sems.at[TILES])
    loading.start()
    gx, gy = lax.axis_index("gx"), lax.axis_index("gy")
    nx, ny = lax.axis_size("gx"), lax.axis_size("gy")
    lane = lane_index()

    def clear(f, carry):
        for c in range(TILES):
            for x in range(X):
                work[c, f, pl.ds(x * 8, 8), :] = jnp.zeros((8, LANES), F32)
        return carry

    lax.fori_loop(0, F, clear, 0)

    def per_code(k, carry):
        from_x, from_y = gx - lax.div(k, 3) + 1, gy - lax.rem(k, 3) + 1
        weight = jnp.where((from_x >= 0) & (from_x < nx) & (from_y >= 0) & (from_y < ny), 1.0, 0.0).astype(F32)
        blocks = [arrived[k, pl.ds(f * 8, 8), :] * weight for f in range(F)]
        for j in range(CAP):
            start = pl.multiple_of(info[k, 2, j] * 8, 8)
            tile = info[k, 3, j]
            hit = lane == info[k, 4, j]
            rows = pl.ds(start, 8)
            held = [work[tile, f, rows, :] for f in range(F)]
            for f in range(F):
                value = jnp.broadcast_to(blocks[f][:, j : j + 1], (8, LANES))
                held[f] = held[f] + jnp.where(hit, value, 0.0)
            for f in range(F):
                work[tile, f, rows, :] = held[f]
        return carry

    lax.fori_loop(0, 9, per_code, 0)
    loading.wait()
    copies = []
    for c in range(TILES):

        def per_field(f, carry):
            for x in range(X):
                rows = pl.ds(x * 8, 8)
                natural[c, f, pl.ds(x, 8, stride=X), :] = section_ref[c, f, rows, :] + work[c, f, rows, :]
            return carry

        lax.fori_loop(0, F, per_field, 0)
        copy = pltpu.make_async_copy(natural.at[c], out_hbm.at[:, :, pl.ds(c * LANES, LANES)], sems.at[c])
        copy.start()
        copies.append(copy)
    for copy in copies:
        copy.wait()


def space(kind, count):
    return [pl.BlockSpec(memory_space=kind)] * count


def shards(conserved, solid_cells, flux_x, flux_y, counts, owner_offset, stencil_base, weights, ghost_cells,
           first_matrix, rest_matrix):
    shape = jax.ShapeDtypeStruct
    u = conserved.reshape(F, Z * X, Y)
    vmem, smem, anywhere = pltpu.VMEM, pltpu.SMEM, pl.ANY
    dma = pltpu.SemaphoreType.DMA
    info = pl.pallas_call(
        prepare_kernel,
        out_shape=shape((9, 8, LANES), I32),
        in_specs=space(smem, 1) + space(vmem, 3),
        out_specs=pl.BlockSpec(memory_space=vmem),
        compiler_params=pltpu.CompilerParams(vmem_limit_bytes=VMEM_BYTES),
        name="prepare",
    )(counts, owner_offset, stencil_base, ghost_cells)
    section, arrived, ghosts = pl.pallas_call(
        main_kernel,
        out_shape=[
            shape((TILES, F, X * Z, LANES), F32), shape((9, F * Z, LANES), F32), shape((9, 8, LANES), I32),
        ],
        in_specs=space(smem, 4) + space(anywhere, 2) + space(vmem, 4) + space(anywhere, 2),
        out_specs=space(anywhere, 3),
        scratch_shapes=[
            pltpu.VMEM((TILES, F, Z * X, LANES), F32),
            pltpu.VMEM((4, 512, 128), BF16), pltpu.VMEM((4, 768, 256), BF16),
            pltpu.VMEM((F, TILES, ROWS, LANES), F32), pltpu.VMEM((768, LANES), F32),
            pltpu.VMEM((ROWS, LANES), F32), pltpu.VMEM((ROWS, LANES), F32),
        ] + [pltpu.VMEM((TILES + 1, ROWS, LANES), BF16)] * 4 + [
            pltpu.VMEM((2, ROWS, 384), F32),
            pltpu.VMEM((7, F, X + 2, Z, LANES), F32), pltpu.VMEM((X + 2, Z, LANES), F32),
            pltpu.VMEM((TILES, F, X * Z, LANES), F32), pltpu.VMEM((9, F * Z, LANES), F32),
        ] + [pltpu.VMEM((F, HALO * 8, Y), F32)] * 2 + [pltpu.VMEM((F, X, LANES), F32)] * 2
        + [pltpu.VMEM((F, HALO * 8, Y), F32)] * 2 + [pltpu.VMEM((F, X, LANES), F32)] * 2
        + [pltpu.VMEM((F, 16, LANES), F32)] * 4
        + [pltpu.VMEM((4, REC, LANES), F32)]
        + [dma((12,)), dma((2, F)), dma((2, F)), dma((15,)), dma((15,)), dma((9,)), dma((9,)), dma((4,))],
        compiler_params=pltpu.CompilerParams(collective_id=0, has_side_effects=True, vmem_limit_bytes=VMEM_BYTES),
        name="section",
    )(
        flux_x, flux_y, counts, info, u, info, owner_offset, stencil_base, weights.T, solid_cells, first_matrix, rest_matrix
    )
    out = pl.pallas_call(
        scatter_kernel,
        out_shape=shape((F, Z * X, Y), F32),
        in_specs=space(smem, 1) + space(anywhere, 1) + space(vmem, 1),
        out_specs=pl.BlockSpec(memory_space=anywhere),
        scratch_shapes=[
            pltpu.VMEM((TILES, F, X * Z, LANES), F32), pltpu.VMEM((TILES, F, X * Z, LANES), F32),
            pltpu.VMEM((TILES, F, Z * X, LANES), F32), dma((TILES + 1,)),
        ],
        compiler_params=pltpu.CompilerParams(vmem_limit_bytes=VMEM_BYTES),
        name="scatter",
    )(ghosts, section, arrived)
    return out.reshape(F, Z, X, Y)


def solution(mesh):
    first, rest = filter_constants()

    def advance(*arguments):
        run = jax.shard_map(
            shards,
            mesh=mesh,
            in_specs=(
                P(None, None, "gx", "gy"), P("gx", "gy"), P(), P(), P(("gx", "gy")), P(("gx", "gy")),
                P(("gx", "gy")), P(("gx", "gy"), None), P(("gx", "gy")), P(), P(),
            ),
            out_specs=P(None, None, "gx", "gy"),
            check_vma=False,
        )
        return run(*arguments, jnp.asarray(first), jnp.asarray(rest))

    return advance
```

```python
import functools

import jax
import jax.numpy as jnp
import ml_dtypes
import numpy as np
from jax import lax
from jax.experimental import pallas as pl
from jax.experimental.pallas import tpu as pltpu
from jax.sharding import PartitionSpec as P

F, Z, X, Y = 5, 8, 64, 512
LANES = 128
TILES = Y // LANES
HALO = 10
EDGE = 24
XE = X + 2 * HALO
ROWS = XE * Z
REC = 576
CAP = 64
SIGNS = (1.0, -1.0, -1.0, -1.0, 1.0)
F32, BF16, I32 = jnp.float32, jnp.bfloat16, jnp.int32
VMEM_BYTES = 60 * 1024 * 1024
OFFSETS = [(k // 3 - 1, k % 3 - 1) for k in range(9)]


def y_matrices(left_edge, right_edge):
    margin = 80
    ys = np.arange(-margin, Y + margin)
    inside = np.ones(ys.shape, bool)
    if left_edge:
        inside &= ys >= 0
    if right_edge:
        inside &= ys < Y
    taps = np.array([1, 6, 15, 20, 15, 6, 1], np.float64) / 64
    single = np.zeros((ys.size, ys.size))
    for offset in range(-3, 4):
        single += np.diag(np.full(ys.size - abs(offset), taps[offset + 3]), offset)
    single = single * inside[:, None] * inside[None, :]
    double = single @ single
    triple = double @ single
    return [-6.0 / 64 * single, 4.0 / 64**2 * double, -1.0 / 64**3 * triple], margin


def block_matrix(powers, margin, y_in, y_out):
    columns = []
    for power in powers:
        full = np.zeros((256, LANES))
        for lane, y in enumerate(y_out):
            if y is not None:
                full[:, lane] = power[y + margin, np.asarray(y_in) + margin]
        columns.append(full)
    return np.concatenate(columns, axis=1)


def filter_constants():
    lane = np.arange(LANES)
    found = []
    for kind in ("mid", "left", "right", "edge_left", "edge_mid", "edge_right"):
        powers, margin = y_matrices(kind.endswith("left"), kind.endswith("right"))
        if kind.startswith("edge"):
            y_in = np.concatenate([np.where(lane < 64, lane, 384 + lane), np.where(lane < 64, Y + lane, lane - 128)])
            y_out = [Y] + [None] * 126 + [-1]
        else:
            c = {"mid": 1, "left": 0, "right": 3}[kind]
            y_in = np.concatenate([128 * c + lane, np.where(lane < 64, 128 * (c + 1) + lane, 128 * (c - 1) + lane)])
            y_out = list(128 * c + lane)
        block = block_matrix(powers, margin, np.clip(y_in, -margin, Y + margin - 1), y_out)
        if kind.startswith("edge"):
            apart = block.reshape(2, LANES, 3, LANES)
            block = sum(np.roll(apart, (EDGE * f, EDGE * f), (1, 3)) for f in range(F)).reshape(256, 3 * LANES)
        found.append(block)
    whole = np.stack(found).astype(np.float32)
    high = whole.astype(ml_dtypes.bfloat16)
    low = (whole - high.astype(np.float32)).astype(ml_dtypes.bfloat16)
    first = np.concatenate([high, high], axis=1)[:, :, :128]
    rest = np.concatenate([high, high, low], axis=1)[:, :, 128:]
    return first, rest


def lane_index(rows=8):
    return lax.broadcasted_iota(I32, (rows, LANES), 1)


ACROSS = (((1,), (1,)), ((), ()))


def place_records(count_ref, code_ref, base_ref):
    code = code_ref[...].reshape(1, REC)
    base = base_ref[...].reshape(1, REC)
    kinds = lax.broadcasted_iota(I32, (16, REC), 0)
    hits = (kinds == code).astype(F32)
    before = (lax.broadcasted_iota(I32, (REC, REC), 0) < lax.broadcasted_iota(I32, (REC, REC), 1)).astype(F32).astype(BF16)
    ahead = jnp.dot(hits.astype(BF16), before, preferred_element_type=F32)
    rank = jnp.sum(ahead * hits, axis=0, keepdims=True).astype(I32)
    slot = code * CAP + rank
    live = lax.broadcasted_iota(I32, (1, REC), 1) < count_ref[0]
    slot = jnp.where(live, slot, REC)
    placing = (lax.broadcasted_iota(I32, (REC, REC), 0) == slot).astype(F32).astype(BF16)
    base_x = ((base.astype(F32) + 0.5) * (1.0 / (Y - 3))).astype(I32)
    base_y = base - base_x * (Y - 3)
    window = jnp.minimum(base_y // 64, 6)
    return placing, window, base_x, base_y - window * 64


def prepare_kernel(count_ref, code_ref, base_ref, ghost_ref, info_ref):
    placing, window, base_x, _ = place_records(count_ref, code_ref, base_ref)
    ghost = ghost_ref[...].reshape(1, REC)
    ghost_y = ghost % Y
    payload_rows = [window, base_x, ghost // Y, ghost_y // LANES, ghost_y % LANES]
    row_id = lax.broadcasted_iota(I32, (8, REC), 0)
    payload = jnp.zeros((8, REC), I32)
    for row, value in enumerate(payload_rows):
        payload = jnp.where(row_id == row, value, payload)
    payload = payload.astype(F32).astype(BF16)
    for k in range(9):
        part = lax.dot_general(payload, placing[k * CAP : (k + 1) * CAP], ACROSS, preferred_element_type=F32)
        info_ref[k] = jnp.concatenate([part, jnp.zeros((8, LANES - CAP), F32)], axis=1).astype(I32)


def spread_weights(count_ref, code_ref, base_ref, weight_ref, wide_ref):
    placing, _, _, first_lane = place_records(count_ref, code_ref, base_ref)
    lanes_hit = (lax.broadcasted_iota(I32, (LANES, REC), 0) == first_lane).astype(F32).astype(BF16)
    starts = lax.dot_general(placing, lanes_hit, ACROSS, preferred_element_type=F32)
    weight = weight_ref[...]
    weight_a = weight.astype(BF16)
    left_over = weight - weight_a.astype(F32)
    weight_b = left_over.astype(BF16)
    weight_c = (left_over - weight_b.astype(F32)).astype(BF16)
    ordered = sum(
        lax.dot_general(placing, part, ACROSS, preferred_element_type=F32) for part in (weight_a, weight_b, weight_c)
    )
    shifted = [starts] + [pltpu.roll(starts, j, 1) for j in range(1, 4)]
    for i in range(4):
        total = shifted[0] * ordered[:, 4 * i : 4 * i + 1]
        for j in range(1, 4):
            total = total + shifted[j] * ordered[:, 4 * i + j : 4 * i + j + 1]
        wide_ref[i] = total


def neighbour(dx, dy):
    nx, ny = lax.axis_size("gx"), lax.axis_size("gy")
    return (lax.rem(lax.axis_index("gx") + dx + nx, nx), lax.rem(lax.axis_index("gy") + dy + ny, ny))


def signal_neighbours():
    barrier = pltpu.get_barrier_semaphore()
    for dx, dy in OFFSETS:
        if (dx, dy) != (0, 0):
            pl.semaphore_signal(barrier, inc=1, device_id=neighbour(dx, dy), device_id_type=pl.DeviceIdType.MESH)


def wait_neighbours():
    pl.semaphore_wait(pltpu.get_barrier_semaphore(), 8)


class Binomial:
    def __init__(self):
        self.held = [None] * 6

    def push(self, value):
        for i in range(6):
            before, self.held[i] = self.held[i], value
            if before is None:
                return None
            value = before + value
        return value


def remote(source, target, send_sem, recv_sem, offset):
    return pltpu.make_async_remote_copy(
        src_ref=source, dst_ref=target, send_sem=send_sem, recv_sem=recv_sem,
        device_id=neighbour(*offset), device_id_type=pl.DeviceIdType.MESH,
    )


def main_kernel(flux_x, flux_y, count_ref, info, u_hbm, info_hbm, code_ref, base_ref, weight_ref, solid_ref, first_hbm, rest_hbm,
                section_hbm, arrived, ghosts,
                ub, firsts, rests, ut, hs, edge_in, edge_out, hi_main, lo_main, hi_side, lo_side, vs, dg, de, section_ref, values_ref,
                low_ref, high_ref, left_ref, right_ref, xlo, xhi, ylo, yhi, cll, clr, chl, chr_,
                wide_ref, sems, row_send, row_recv, side_send, side_recv, record_send, record_recv, out_sems):
    signal_neighbours()
    gx, gy = lax.axis_index("gx"), lax.axis_index("gy")
    last_x, last_y = lax.axis_size("gx") - 1, lax.axis_size("gy") - 1
    flag_lo = jnp.where(gx > 0, 1.0, 0.0).astype(F32)
    flag_hi = jnp.where(gx < last_x, 1.0, 0.0).astype(F32)
    flag_left = jnp.where(gy > 0, 1.0, 0.0).astype(F32)
    flag_right = jnp.where(gy < last_y, 1.0, 0.0).astype(F32)
    kinds = [
        jnp.where(gy == 0, 1, 0),
        0,
        jnp.where(gy == last_y, 2, 0),
        jnp.where(gy == 0, 3, jnp.where(gy == last_y, 5, 4)),
    ]
    copies = [
        pltpu.make_async_copy(u_hbm.at[:, :, pl.ds(c * LANES, LANES)], ub.at[c], sems.at[c]) for c in range(TILES)
    ]
    constant_copies = []
    for i, kind in enumerate(kinds):
        constant_copies.append(pltpu.make_async_copy(first_hbm.at[kind], firsts.at[i], sems.at[4 + i]))
        constant_copies.append(pltpu.make_async_copy(rest_hbm.at[kind], rests.at[i], sems.at[8 + i]))
    for copy in [copies[0], copies[3], copies[1], copies[2]] + constant_copies:
        copy.start()
    copies[0].wait()
    copies[3].wait()
    lane = lane_index()
    low_half = lane < 64

    def pack_sides(f, carry):
        for octet in range(8):
            left = jnp.zeros((8, LANES), F32)
            right = jnp.zeros((8, LANES), F32)
            for z in range(Z):
                here = (lane // 16) == z
                row = z * X + octet * 8
                left = jnp.where(here, pltpu.roll(ub[0, f, pl.ds(row, 8), :], 16 * z, 1), left)
                right = jnp.where(
                    here, pltpu.roll(ub[TILES - 1, f, pl.ds(row, 8), :], (16 * z - (LANES - HALO)) % LANES, 1), right
                )
            left_ref[f, pl.ds(octet * 8, 8), :] = left
            right_ref[f, pl.ds(octet * 8, 8), :] = right
        return carry

    lax.fori_loop(0, F, pack_sides, 0)
    wait_neighbours()
    plan = [
        (right_ref, ylo, (0, 1)),
        (left_ref, yhi, (0, -1)),
        (right_ref.at[:, pl.ds(X - 16, 16)], cll, (1, 1)),
        (left_ref.at[:, pl.ds(X - 16, 16)], clr, (1, -1)),
        (right_ref.at[:, pl.ds(0, 16)], chl, (-1, 1)),
        (left_ref.at[:, pl.ds(0, 16)], chr_, (-1, -1)),
    ]
    side_copies = [
        remote(source, target, side_send.at[index], side_recv.at[index], offset)
        for index, (source, target, offset) in enumerate(plan)
    ]
    for copy in side_copies:
        copy.start()

    copies[1].wait()
    copies[2].wait()

    def pack_rows(f, carry):
        for c in range(TILES):
            for x in range(HALO):
                low_ref[f, pl.ds(x * 8, 8), pl.ds(c * LANES, LANES)] = ub[c, f, pl.ds(x, 8, stride=X), :]
                high_ref[f, pl.ds(x * 8, 8), pl.ds(c * LANES, LANES)] = ub[c, f, pl.ds(X - HALO + x, 8, stride=X), :]
        return carry

    lax.fori_loop(0, F, pack_rows, 0)
    def row_copies(f):
        return (
            remote(high_ref.at[f], xlo.at[f], row_send.at[0, f], row_recv.at[0, f], (1, 0)),
            remote(low_ref.at[f], xhi.at[f], row_send.at[1, f], row_recv.at[1, f], (-1, 0)),
        )

    for f in range(F):
        for copy in row_copies(f):
            copy.start()

    spread_weights(count_ref, code_ref, base_ref, weight_ref, wide_ref)
    ghost_copies = [
        remote(info_hbm.at[k], ghosts.at[k], side_send.at[6 + k], side_recv.at[6 + k], offset)
        for k, offset in enumerate(OFFSETS) if k != 4
    ]
    for copy in ghost_copies:
        copy.start()
    own_ghosts = pltpu.make_async_copy(info_hbm.at[4], ghosts.at[4], out_sems.at[0])
    own_ghosts.start()

    def turn(f, carry):
        for c in range(TILES):
            for x in range(X):
                ut[f, c, pl.ds((HALO + x) * 8, 8), :] = ub[c, f, pl.ds(x, 8, stride=X), :]
        return carry

    lax.fori_loop(0, F, turn, 0)
    for copy in constant_copies:
        copy.wait()
    for copy in side_copies:
        copy.wait_recv()

    def filter_block(c, which, f):
        high = jnp.concatenate([hi_main[c], hi_side[c]], axis=1)
        low = jnp.concatenate([lo_main[c], lo_side[c]], axis=1)
        vs[c % 2, :, pl.ds(0, 128)] = jnp.dot(
            jnp.concatenate([high, low], axis=1), firsts[which], preferred_element_type=F32
        )
        vs[c % 2, :, pl.ds(128, 256)] = jnp.dot(
            jnp.concatenate([high, low, high], axis=1), rests[which], preferred_element_type=F32
        )
        stages = [Binomial(), Binomial(), Binomial()]

        def mask(value, e):
            return value * flag_lo if e < HALO else value * flag_hi if e >= HALO + X else value

        for e in range(XE):
            value = stages[2].push(vs[c % 2, pl.ds(e * 8, 8), pl.ds(256, 128)])
            if value is None:
                continue
            value = mask(value, e - 3) + vs[c % 2, pl.ds((e - 3) * 8, 8), pl.ds(128, 128)]
            value = stages[1].push(value)
            if value is None:
                continue
            value = mask(value, e - 6) + vs[c % 2, pl.ds((e - 6) * 8, 8), pl.ds(0, 128)]
            value = stages[0].push(value)
            if value is None:
                continue
            at = e - 9
            start = ut[f, c, pl.ds(at * 8, 8), :] if c < TILES else edge_out[pl.ds(at * 8, 8), :]
            value = mask(value, at) + 4.0 * start
            if c == TILES:
                de[at - 9] = value
            else:
                dg[2 * c, f, at - 9] = value

    def clear_edges(e, carry):
        rows = pl.ds(pl.multiple_of(e * 8, 8), 8)
        edge_in[rows, :] = jnp.zeros((8, LANES), F32)
        edge_out[rows, :] = jnp.zeros((8, LANES), F32)
        return carry

    lax.fori_loop(0, XE, clear_edges, 0)

    def per_field(f, carry):
        for copy in row_copies(f):
            copy.wait_recv()
        for c in range(TILES):
            ut[f, c, pl.ds(0, 80), :] = xlo[f, :, pl.ds(c * LANES, LANES)] * flag_lo
            ut[f, c, pl.ds(ROWS - 80, 80), :] = xhi[f, :, pl.ds(c * LANES, LANES)] * flag_hi
        for octet in range(-2, 10):
            if octet < 0:
                left, right = [r[f, pl.ds((octet + 2) * 8, 8), :] * flag_lo for r in (cll, clr)]
            elif octet >= 8:
                left, right = [r[f, pl.ds((octet - 8) * 8, 8), :] * flag_hi for r in (chl, chr_)]
            else:
                left, right = [r[f, pl.ds(octet * 8, 8), :] for r in (ylo, yhi)]
            left, right = left * flag_left, right * flag_right
            for z in range(Z):
                from_right = pltpu.roll(right, (-16 * z) % LANES, 1)
                from_left = pltpu.roll(left, (LANES - HALO - 16 * z) % LANES, 1)
                hs[pl.ds((octet + 2) * 64 + z, 8, stride=8), :] = jnp.where(low_half, from_right, from_left)

        window = ((lane - EDGE * f + EDGE // 2) & (LANES - 1)) < EDGE
        for e in range(XE):
            rows = pl.ds(e * 8, 8)
            inner = jnp.where(low_half, ut[f, 0, rows, :], ut[f, TILES - 1, rows, :])
            edge_in[rows, :] = jnp.where(window, pltpu.roll(inner, EDGE * f, 1), edge_in[rows, :])
            outer = hs[pl.ds(e * 8 + 48, 8), :]
            edge_out[rows, :] = jnp.where(window, pltpu.roll(outer, EDGE * f, 1), edge_out[rows, :])

        keep_low = (lane_index(16) < 64).astype(F32).astype(BF16)
        keep_high = (lane_index(16) >= 64).astype(F32).astype(BF16)
        for block in range(ROWS // 16):
            rows = pl.ds(block * 16, 16)
            highs, lows = [], []
            for c in range(TILES + 1):
                value = ut[f, c, rows, :] if c < TILES else hs[pl.ds(block * 16 + 48, 16), :]
                high = value.astype(BF16)
                low = (value - high.astype(F32)).astype(BF16)
                highs.append(high)
                lows.append(low)
            for parts, main, side in ((highs, hi_main, hi_side), (lows, lo_main, lo_side)):
                lo_parts = [p * keep_low for p in parts]
                hi_parts = [p * keep_high for p in parts]
                for c in range(TILES):
                    main[c, rows, :] = parts[c]
                    after = lo_parts[c + 1] if c < TILES - 1 else lo_parts[TILES]
                    ahead = hi_parts[c - 1] if c > 0 else hi_parts[TILES]
                    side[c, rows, :] = after + ahead

        for c in range(TILES):
            filter_block(c, (0, 1, 1, 2)[c], f)
        for x in range(1, X + 1):
            turned = [pltpu.roll(dg[2 * c, f, x], 64, 1) for c in range(TILES)]
            for c in range(TILES - 1):
                dg[2 * c + 1, f, x] = jnp.where(low_half, turned[c], turned[c + 1])
        return carry

    lax.fori_loop(0, F, per_field, 0)
    for block in range(ROWS // 16):
        rows = pl.ds(block * 16, 16)
        for source, high_ref_, low_ref_ in ((edge_in, hi_main, lo_main), (edge_out, hi_side, lo_side)):
            high = source[rows, :].astype(BF16)
            high_ref_[TILES, rows, :] = high
            low_ref_[TILES, rows, :] = (source[rows, :] - high.astype(F32)).astype(BF16)
    filter_block(TILES, 3, 0)

    def record_copy(k):
        offset = (lax.div(k, 3) - 1, lax.rem(k, 3) - 1)
        return remote(values_ref.at[k], arrived.at[k], record_send.at[k], record_recv.at[k], offset)

    def per_code(k, carry):
        held = [jnp.zeros((8, LANES), F32) for _ in range(F)]
        for group in range(CAP // 8):
            weights = [wide_ref[i, pl.ds(pl.multiple_of(k * CAP + group * 8, 8), 8), :] for i in range(4)]
            for j in range(8):
                slot = group * 8 + j
                window = info[k, 0, slot]
                start = info[k, 1, slot] + 1
                rows = [jnp.broadcast_to(weights[i][j : j + 1, :], (8, LANES)) for i in range(4)]
                for f in range(F):
                    total = dg[window, f, start] * rows[0]
                    for i in range(1, 4):
                        total = total + dg[window, f, start + i] * rows[i]
                    value = jnp.sum(total, axis=1, keepdims=True) * SIGNS[f]
                    held[f] = jnp.where(lane == slot, value, held[f])
        for f in range(F):
            values_ref[k, pl.ds(f * 8, 8), :] = held[f]

        @pl.when(k != 4)
        def _():
            record_copy(k).start()

        return carry

    lax.fori_loop(0, 9, per_code, 0)
    own_values = pltpu.make_async_copy(values_ref.at[4], arrived.at[4], out_sems.at[1])
    own_values.start()

    mix_x = [[flux_x[f, g] * -0.125 for g in range(F)] for f in range(F)]
    mix_y = [[flux_y[f, g] * -0.125 for g in range(F)] for f in range(F)]

    def per_octet(octet, carry):
        for c in range(TILES):
            solid = solid_ref[pl.ds(pl.multiple_of(octet * 8, 8), 8), pl.ds(c * LANES, LANES)]
            for half in range(4):
                first = octet * 8 + half * 2
                here = pl.ds(first + 1, 2)
                slopes_x, slopes_y, mids = [], [], []
                wide_lane = lax.broadcasted_iota(I32, (2, 8, LANES), 2)
                for g in range(F):
                    mid = dg[2 * c, g, here]
                    before = dg[2 * c, g, pl.ds(first, 2)]
                    after = dg[2 * c, g, pl.ds(first + 2, 2)]
                    left = dg[2 * (c - 1), g, here] if c > 0 else de[here]
                    right = dg[2 * (c + 1), g, here] if c < TILES - 1 else de[here]
                    left_turn = 1 if c > 0 else (1 - EDGE * g) % LANES
                    right_turn = LANES - 1 if c < TILES - 1 else (LANES - 1 - EDGE * g) % LANES
                    up = jnp.where(wide_lane == LANES - 1, pltpu.roll(right, right_turn, 2), pltpu.roll(mid, LANES - 1, 2))
                    down = jnp.where(wide_lane == 0, pltpu.roll(left, left_turn, 2), pltpu.roll(mid, 1, 2))
                    mids.append(mid)
                    slopes_x.append(after - before)
                    slopes_y.append(up - down)
                for f in range(F):
                    total = -0.125 * mids[f]
                    for g in range(F):
                        total = total + mix_x[f][g] * slopes_x[g] + mix_y[f][g] * slopes_y[g]
                    for i in range(2):
                        x = octet * 8 + half * 2 + i
                        cells = total[i] + 1.125 * ut[f, c, pl.ds(pl.multiple_of((x + HALO) * 8, 8), 8), :]
                        row = half * 2 + i
                        blocked = jnp.broadcast_to(solid[row : row + 1, :], (8, LANES)) == 1
                        section_ref[c, f, pl.ds(pl.multiple_of((first + i) * 8, 8), 8), :] = jnp.where(blocked, 0.0, cells)
        return carry

    written = []
    for half in range(4):
        lax.fori_loop(half * 2, half * 2 + 2, per_octet, 0)
        rows = pl.ds(half * 128, 128)
        written.append(
            pltpu.make_async_copy(section_ref.at[:, :, rows], section_hbm.at[:, :, rows], out_sems.at[2 + half])
        )
        written[-1].start()

    def finish_field(f, carry):
        for copy in row_copies(f):
            copy.wait_send()
        return carry

    lax.fori_loop(0, F, finish_field, 0)
    for copy in side_copies:
        copy.wait_send()
    for copy in ghost_copies:
        copy.wait()
    for k in range(9):
        if k != 4:
            record_copy(k).wait()
    for copy in written + [own_ghosts, own_values]:
        copy.wait()


def scatter_kernel(info, section_hbm, arrived, out_hbm, section_ref, work, natural, sems):
    loading = pltpu.make_async_copy(section_hbm, section_ref, sems.at[TILES])
    loading.start()
    gx, gy = lax.axis_index("gx"), lax.axis_index("gy")
    nx, ny = lax.axis_size("gx"), lax.axis_size("gy")
    lane = lane_index()

    def clear(f, carry):
        for c in range(TILES):
            for x in range(X):
                work[c, f, pl.ds(x * 8, 8), :] = jnp.zeros((8, LANES), F32)
        return carry

    lax.fori_loop(0, F, clear, 0)

    def per_code(k, carry):
        from_x, from_y = gx - lax.div(k, 3) + 1, gy - lax.rem(k, 3) + 1
        weight = jnp.where((from_x >= 0) & (from_x < nx) & (from_y >= 0) & (from_y < ny), 1.0, 0.0).astype(F32)
        blocks = [arrived[k, pl.ds(f * 8, 8), :] * weight for f in range(F)]
        for j in range(CAP):
            start = pl.multiple_of(info[k, 2, j] * 8, 8)
            tile = info[k, 3, j]
            hit = lane == info[k, 4, j]
            rows = pl.ds(start, 8)
            held = [work[tile, f, rows, :] for f in range(F)]
            for f in range(F):
                value = jnp.broadcast_to(blocks[f][:, j : j + 1], (8, LANES))
                held[f] = held[f] + jnp.where(hit, value, 0.0)
            for f in range(F):
                work[tile, f, rows, :] = held[f]
        return carry

    lax.fori_loop(0, 9, per_code, 0)
    loading.wait()
    copies = []
    for c in range(TILES):

        def per_field(f, carry):
            for x in range(X):
                rows = pl.ds(x * 8, 8)
                natural[c, f, pl.ds(x, 8, stride=X), :] = section_ref[c, f, rows, :] + work[c, f, rows, :]
            return carry

        lax.fori_loop(0, F, per_field, 0)
        copy = pltpu.make_async_copy(natural.at[c], out_hbm.at[:, :, pl.ds(c * LANES, LANES)], sems.at[c])
        copy.start()
        copies.append(copy)
    for copy in copies:
        copy.wait()


def space(kind, count):
    return [pl.BlockSpec(memory_space=kind)] * count


def shards(conserved, solid_cells, flux_x, flux_y, counts, owner_offset, stencil_base, weights, ghost_cells,
           first_matrix, rest_matrix):
    shape = jax.ShapeDtypeStruct
    u = conserved.reshape(F, Z * X, Y)
    vmem, smem, anywhere = pltpu.VMEM, pltpu.SMEM, pl.ANY
    dma = pltpu.SemaphoreType.DMA
    info = pl.pallas_call(
        prepare_kernel,
        out_shape=shape((9, 8, LANES), I32),
        in_specs=space(smem, 1) + space(vmem, 3),
        out_specs=pl.BlockSpec(memory_space=vmem),
        compiler_params=pltpu.CompilerParams(vmem_limit_bytes=VMEM_BYTES),
        name="prepare",
    )(counts, owner_offset, stencil_base, ghost_cells)
    section, arrived, ghosts = pl.pallas_call(
        main_kernel,
        out_shape=[
            shape((TILES, F, X * Z, LANES), F32), shape((9, F * Z, LANES), F32), shape((9, 8, LANES), I32),
        ],
        in_specs=space(smem, 4) + space(anywhere, 2) + space(vmem, 4) + space(anywhere, 2),
        out_specs=space(anywhere, 3),
        scratch_shapes=[
            pltpu.VMEM((TILES, F, Z * X, LANES), F32),
            pltpu.VMEM((4, 512, 128), BF16), pltpu.VMEM((4, 768, 256), BF16),
            pltpu.VMEM((F, TILES, ROWS, LANES), F32), pltpu.VMEM((768, LANES), F32),
            pltpu.VMEM((ROWS, LANES), F32), pltpu.VMEM((ROWS, LANES), F32),
        ] + [pltpu.VMEM((TILES + 1, ROWS, LANES), BF16)] * 4 + [
            pltpu.VMEM((2, ROWS, 384), F32),
            pltpu.VMEM((7, F, X + 2, Z, LANES), F32), pltpu.VMEM((X + 2, Z, LANES), F32),
            pltpu.VMEM((TILES, F, X * Z, LANES), F32), pltpu.VMEM((9, F * Z, LANES), F32),
        ] + [pltpu.VMEM((F, HALO * 8, Y), F32)] * 2 + [pltpu.VMEM((F, X, LANES), F32)] * 2
        + [pltpu.VMEM((F, HALO * 8, Y), F32)] * 2 + [pltpu.VMEM((F, X, LANES), F32)] * 2
        + [pltpu.VMEM((F, 16, LANES), F32)] * 4
        + [pltpu.VMEM((4, REC, LANES), F32)]
        + [dma((12,)), dma((2, F)), dma((2, F)), dma((15,)), dma((15,)), dma((9,)), dma((9,)), dma((6,))],
        compiler_params=pltpu.CompilerParams(collective_id=0, has_side_effects=True, vmem_limit_bytes=VMEM_BYTES),
        name="section",
    )(
        flux_x, flux_y, counts, info, u, info, owner_offset, stencil_base, weights.T, solid_cells, first_matrix, rest_matrix
    )
    out = pl.pallas_call(
        scatter_kernel,
        out_shape=shape((F, Z * X, Y), F32),
        in_specs=space(smem, 1) + space(anywhere, 1) + space(vmem, 1),
        out_specs=pl.BlockSpec(memory_space=anywhere),
        scratch_shapes=[
            pltpu.VMEM((TILES, F, X * Z, LANES), F32), pltpu.VMEM((TILES, F, X * Z, LANES), F32),
            pltpu.VMEM((TILES, F, Z * X, LANES), F32), dma((TILES + 1,)),
        ],
        compiler_params=pltpu.CompilerParams(vmem_limit_bytes=VMEM_BYTES),
        name="scatter",
    )(ghosts, section, arrived)
    return out.reshape(F, Z, X, Y)


def solution(mesh):
    first, rest = filter_constants()

    def advance(*arguments):
        run = jax.shard_map(
            shards,
            mesh=mesh,
            in_specs=(
                P(None, None, "gx", "gy"), P("gx", "gy"), P(), P(), P(("gx", "gy")), P(("gx", "gy")),
                P(("gx", "gy")), P(("gx", "gy"), None), P(("gx", "gy")), P(), P(),
            ),
            out_specs=P(None, None, "gx", "gy"),
            check_vma=False,
        )
        return run(*arguments, jnp.asarray(first), jnp.asarray(rest))

    return advance
```
